512 devices in a mesh: lon: 64 (over y_hi, z, core), lat: 8 (over y_lo, x).
Axes of the slice: x: 4, y: 8 (y_hi: 4, y_lo: 2; y = y_hi * 2 + y_lo), z: 8, core: 2. Of those that a mesh axis runs over, the one named last changes fastest.
Arguments:
- state: bfloat16 [216, 8, 192, 1024], P(None, None, 'lon', 'lat'), may hold values from -6 to 6
- adjoint: bfloat16 [216, 8, 192, 1024], P(None, None, 'lon', 'lat'), may hold values from -6 to 6
- derivative: bfloat16 [3, 216, 216], replicated, may hold values from -0.25 to 0.25
- jac_tensor: bfloat16 [3, 8, 8, 8], replicated, may hold values from -2 to 2
- jac_offset: bfloat16 [3, 8, 8], replicated, may hold values from -2 to 2
- zonal_kernel: float32 [192], replicated, may hold values from -6 to 6
- face_numbers: int32 [192, 1024, 6], P('lon', 'lat'), may hold values from 0 to 5, each once within a row
- orientation: int32 [192, 1024, 6], P('lon', 'lat'), may hold values from 0 to 7
Outputs:
- gradient: bfloat16 [216, 8, 192, 1024], P(None, None, 'lon', 'lat')
The draws below stay inside these ranges and needn't reach their ends.
Inputs may be any that keep to these rules, and one draw needn't show every extreme that they name: `face_numbers`: the six entries of each element are the local faces 0 to 5, each once.
All inputs are finite; a program needn't handle non-finite values.
Results may differ from the reference program's by a relative error of at most 0.0051.
Values may be sent and summed in bfloat16 or wider, within the bound.
A program may use at most 128 MiB of HBM per device.

```python
import jax
import jax.numpy as jnp
from jax import lax

NODES1 = 6
NODES = 216
FIELDS = 8
ERAD = 64
LONS = 192
COLS = 1024


def with_ends(drawn, stream_key, low, top_value):
    longest = drawn.shape.index(max(drawn.shape))
    spots = []
    for shift in (0, 1):
        where = [jax.random.randint(jax.random.fold_in(stream_key, axis), (), 0, length) for axis, length in enumerate(drawn.shape)]
        where[longest] = (where[longest] + shift) % drawn.shape[longest]
        spots.append(tuple(where))
    return drawn.at[spots[0]].set(low).at[spots[1]].set(top_value)


def levels(stream_key, shape, cuts, least, top_value):
    def one(dim, shards_of):
        draws = jax.random.uniform(jax.random.fold_in(jax.random.fold_in(stream_key, 6), dim), (shards_of,), jnp.float32, least / len(cuts), top_value / len(cuts))
        return jnp.repeat(jnp.exp(draws), shape[dim] // shards_of).reshape((-1,) + (1,) * (len(shape) - dim - 1))

    loudness = one(*cuts[0])
    for cut in cuts[1:]:
        loudness = loudness * one(*cut)
    return loudness


def normal_values(own_key, shape, width, bound, cuts=(), kind=jnp.bfloat16):
    array = jax.random.normal(own_key, shape, jnp.float32) * width
    if len(cuts) > 0:
        array = levels(own_key, shape, cuts, -0.22, 0.18) * array
    return jnp.clip(array, min=-bound, max=bound).astype(kind)


def setup_inputs(seed: int = 0) -> dict:
    key_list = jax.random.split(jax.random.key(seed), 9)
    state = normal_values(key_list[0], (NODES, FIELDS, LONS, COLS), 1.0, 6.0, ((2, 64), (3, 8)))
    adjoint = normal_values(key_list[1], (NODES, FIELDS, LONS, COLS), 1.0, 6.0, ((2, 64), (3, 8)))
    derivative = normal_values(key_list[2], (3, NODES, NODES), (3 * NODES) ** -0.5, 0.25)
    jac_tensor = normal_values(key_list[3], (3, FIELDS, FIELDS, FIELDS), FIELDS ** -0.5, 2.0)
    jac_offset = normal_values(key_list[4], (3, FIELDS, FIELDS), FIELDS ** -0.5, 2.0)
    zonal_kernel = normal_values(key_list[5], (LONS,), 1.0, 6.0, (), jnp.float32)
    face_numbers = jax.vmap(lambda own: jax.random.permutation(own, 6))(jax.random.split(key_list[6], LONS * COLS)).reshape((LONS, COLS, 6)).astype(jnp.int32)
    orientation = with_ends(jax.random.randint(key_list[7], (LONS, COLS, 6), 0, 8), jax.random.fold_in(key_list[7], 1), 0, 7).astype(jnp.int32)
    return {"state": state, "adjoint": adjoint, "derivative": derivative, "jac_tensor": jac_tensor, "jac_offset": jac_offset, "zonal_kernel": zonal_kernel, "face_numbers": face_numbers, "orientation": orientation}


HIGHEST_PRECISION = lax.Precision.HIGHEST

def coefficients(jac_tensor, jac_offset):
    fields = jac_tensor.shape[1]
    quadratic = jnp.transpose(jac_tensor, (0, 2, 1, 3)).reshape((3, fields, fields * fields))
    linear = jnp.transpose(jac_offset, (0, 2, 1))
    return jnp.concatenate([quadratic, linear], axis=2)

def bilinear_input(state_part, weight_part):
    extent, fields, amount = state_part.shape
    product = (weight_part[:, :, None, :] * state_part[:, None, :, :]).reshape((extent, fields * fields, amount))
    return jnp.concatenate([product, weight_part], axis=1).astype(jnp.bfloat16)

def volume_block(weights_all, derivative, state_block, adjoint_block):
    nodes, fields, amount = state_block.shape
    inputs = bilinear_input(state_block.astype(jnp.float32), adjoint_block.astype(jnp.float32))
    transposed = jnp.einsum('dbx,pxm->dpbm', weights_all.astype(jnp.float32), inputs.astype(jnp.float32), precision=HIGHEST_PRECISION).astype(jnp.bfloat16)
    flattened = transposed.reshape((3 * nodes, fields * amount))
    stacked = derivative.reshape((3 * nodes, nodes))
    result = lax.dot_general(stacked, flattened, (((0,), (0,)), ((), ())), preferred_element_type=jnp.float32)
    return result.reshape((nodes, fields, amount))

def face_planes(blocks):
    return jnp.stack([blocks[:, :, 0], blocks[:, :, -1], blocks[:, 0], blocks[:, -1], blocks[0], blocks[-1]], axis=0)

def lift_planes(planes, blocks):
    blocks = blocks.at[:, :, 0].add(planes[0])
    blocks = blocks.at[:, :, -1].add(planes[1])
    blocks = blocks.at[:, 0].add(planes[2])
    blocks = blocks.at[:, -1].add(planes[3])
    blocks = blocks.at[0].add(planes[4])
    blocks = blocks.at[-1].add(planes[5])
    return blocks

def select_faces(planes, numbers):
    chosen = []
    for direction in range(6):
        picked = jnp.zeros_like(planes[0])
        for number in range(6):
            picked = jnp.where(numbers[..., direction] == number, planes[number], picked)
        chosen.append(picked)
    return jnp.stack(chosen, axis=0)

def return_faces(contributions, numbers):
    placed = []
    for number in range(6):
        picked = jnp.zeros_like(contributions[0])
        for direction in range(6):
            picked = jnp.where(numbers[..., direction] == number, contributions[direction], picked)
        placed.append(picked)
    return jnp.stack(placed, axis=0)

def orient_face(remote, turnings):
    result = remote
    for variant in range(1, 8):
        turned = remote
        if variant & 1:
            turned = jnp.swapaxes(turned, 0, 1)
        if variant & 2:
            turned = turned[::-1]
        if variant & 4:
            turned = turned[:, ::-1]
        result = jnp.where(turnings == variant, turned, result)
    return result

def face_flux(weights, normal_sign, own_values, remote, fields):
    layout = own_values.shape
    extent = layout[0] * layout[1]
    own_flat = own_values.astype(jnp.float32).reshape((extent, layout[2], -1))
    remote_flat = remote.astype(jnp.float32).reshape((extent, layout[2], -1))
    state_left = own_flat[:, :fields]
    adjoint_left = own_flat[:, fields:]
    state_right = remote_flat[:, :fields]
    adjoint_right = remote_flat[:, fields:]
    jump_adjoint = adjoint_left - adjoint_right
    paired = bilinear_input(state_left, jump_adjoint)
    applied = jnp.einsum('bx,rxm->rbm', weights.astype(jnp.float32), paired.astype(jnp.float32), precision=HIGHEST_PRECISION)
    speed_left = jnp.sqrt(1.0 + lax.optimization_barrier(jnp.sum(state_left * state_left, axis=1, keepdims=True)))
    speed_right = jnp.sqrt(1.0 + lax.optimization_barrier(jnp.sum(state_right * state_right, axis=1, keepdims=True)))
    penalty = 0.5 * (speed_left + speed_right)
    jump_state = lax.optimization_barrier(jnp.sum((state_right - state_left) * jump_adjoint, axis=1, keepdims=True))
    flux_term = 0.5 * normal_sign * applied + 0.5 * penalty * jump_adjoint - 0.25 * jump_state * state_left / speed_left
    return flux_term.reshape((layout[0], layout[1], fields) + layout[3:])

def reference(state, adjoint, derivative, jac_tensor, jac_offset, zonal_kernel, face_numbers, orientation):
    weights_all = coefficients(jac_tensor, jac_offset)
    fields = FIELDS
    columns = COLS
    means = lax.optimization_barrier(jnp.sum(adjoint, axis=0, dtype=jnp.float32)) / NODES
    everything = jnp.arange(LONS, dtype=jnp.int32)
    offsets = (everything[:, None] - everything[None, :]) % LONS
    circulant = zonal_kernel[offsets]
    zonal = jnp.einsum('lk,bkc->blc', circulant, means, precision=HIGHEST_PRECISION)
    grid_shape = (NODES1, NODES1, 2 * fields, columns // ERAD, ERAD)

    def slice_traces(longitude):
        joined = jnp.concatenate([state[:, :, longitude, :], adjoint[:, :, longitude, :]], axis=1)
        blocks = joined.reshape((NODES1, NODES1, NODES1, 2 * fields, columns))
        return select_faces(face_planes(blocks), face_numbers[longitude])

    def move_rows(portion, axis_number, forward):
        grid = portion.reshape(grid_shape)
        length = grid.shape[axis_number]
        blank = jnp.zeros_like(lax.slice_in_dim(grid, 0, 1, axis=axis_number))
        if forward:
            grid = jnp.concatenate([blank, lax.slice_in_dim(grid, 0, length - 1, axis=axis_number)], axis=axis_number)
        else:
            grid = jnp.concatenate([lax.slice_in_dim(grid, 1, length, axis=axis_number), blank], axis=axis_number)
        return grid.reshape(portion.shape)

    def one_longitude(longitude):
        western = (longitude + LONS - 1) % LONS
        eastern = (longitude + 1) % LONS
        own_traces = slice_traces(longitude)
        remotes = [slice_traces(western)[1], slice_traces(eastern)[0], move_rows(own_traces[3], 3, True), move_rows(own_traces[2], 3, False), move_rows(own_traces[5], 4, True), move_rows(own_traces[4], 4, False)]
        contributions = []
        for direction in range(6):
            remote = orient_face(remotes[direction], orientation[longitude][:, direction])
            normal_sign = 2.0 * (direction % 2) - 1.0
            contributions.append(face_flux(weights_all[direction // 2], normal_sign, own_traces[direction], remote, fields))
        placed = return_faces(jnp.stack(contributions, axis=0), face_numbers[longitude])
        blocks = lift_planes(placed, jnp.zeros((NODES1, NODES1, NODES1, fields, columns), jnp.float32))
        lifted = blocks.reshape((NODES, fields, columns))
        volume = volume_block(weights_all, derivative, state[:, :, longitude, :], adjoint[:, :, longitude, :])
        gradient_sum = volume + lifted + zonal[:, longitude, :][None]
        return gradient_sum.astype(jnp.bfloat16)
    result = lax.map(one_longitude, jnp.arange(LONS, dtype=jnp.int32))
    return jnp.moveaxis(result, 0, 2)
```

```python
import functools

import jax
import jax.numpy as jnp
from jax import lax
from jax.experimental import pallas as pl
from jax.experimental.pallas import tpu as pltpu
from jax.sharding import PartitionSpec as P

MESH = pl.DeviceIdType.MESH
F32 = jnp.float32
BF16 = jnp.bfloat16
HIGH = lax.Precision.HIGHEST
PAIRS = 14
NETWORK = [(0, 5), (1, 3), (2, 4), (1, 2), (3, 4), (0, 3), (2, 5), (0, 1), (2, 3), (4, 5), (1, 2), (3, 4)]
VMEM_LIMIT = 56 * 1024 * 1024


def iota(shape, axis):
    return lax.broadcasted_iota(jnp.int32, shape, axis)


def onehot(condition):
    return condition.astype(F32).astype(BF16)


def fill_swaps(numbers_ref, swaps):
    for t in range(3):
        keys = [jnp.broadcast_to(numbers_ref[t, g : g + 1, :], (8, 128)) for g in range(6)]
        for step, (i, j) in enumerate(NETWORK):
            swaps[t, step] = (keys[i] > keys[j]).astype(jnp.int32)
            keys[i], keys[j] = jnp.minimum(keys[i], keys[j]), jnp.maximum(keys[i], keys[j])


def face_node(face, u, v):
    if face < 2:
        return u * 36 + v * 6 + 5 * face
    if face < 4:
        return u * 36 + 30 * (face - 2) + v
    return 180 * (face - 4) + u * 6 + v


def select_own(s_ref, a_ref, swaps, own):
    def step(index, carry):
        t = index // 6
        u = index % 6
        for v in range(6):
            ss, aa = [], []
            for face in range(6):
                q = face_node(face, u, v)
                ss.append(s_ref[q, t].astype(F32))
                aa.append(a_ref[q, t].astype(F32))
            for s in range(len(NETWORK) - 1, -1, -1):
                i, j = NETWORK[s]
                swap = swaps[t, s] != 0
                ss[i], ss[j] = jnp.where(swap, ss[j], ss[i]), jnp.where(swap, ss[i], ss[j])
                aa[i], aa[j] = jnp.where(swap, aa[j], aa[i]), jnp.where(swap, aa[i], aa[j])
            for g in range(6):
                own[g, t, u * 6 + v] = jnp.concatenate([ss[g], aa[g]], axis=0).astype(BF16)
        return carry

    lax.fori_loop(0, 18, step, 0)


def volume_weights(jac_ref, off_ref, wv):
    jac2 = jac_ref[...].astype(BF16)
    spread = onehot((iota((8, 512), 1) & 7) == iota((8, 512), 0))
    x = jnp.dot(jac2, spread, preferred_element_type=F32)
    row = iota((192, 512), 0)
    col = iota((192, 512), 1)
    x = jnp.where(((col >> 3) & 7) == ((row >> 3) & 7), x, 0.0).astype(BF16)
    r = iota((192, 192), 0)
    c = iota((192, 192), 1)
    r8 = r >> 3
    rb = jnp.zeros_like(r8)
    for b in range(1, 8):
        rb = rb + (r8 >= 3 * b).astype(jnp.int32)
    rd = r8 - 3 * rb
    pick = onehot(((c >> 6) == rd) & ((c & 7) == rb))
    y = jnp.dot(pick, x, preferred_element_type=F32)
    wv[:, 0:512] = jnp.where((col >> 6) == (row & 7), y, 0.0).astype(BF16)
    rb8 = rb[:, 0:8]
    gb = onehot(iota((192, 8), 1) == rb8)
    z = lax.dot_general(gb, off_ref[...], (((1,), (1,)), ((), ())), preferred_element_type=F32)
    rd24 = rd[:, 0:24]
    z = jnp.where((iota((192, 24), 1) >> 3) == rd24, z, 0.0).astype(BF16)
    place = onehot((iota((24, 64), 0) & 7) == (iota((24, 64), 1) & 7))
    lin = jnp.dot(z, place, preferred_element_type=F32)
    wv[:, 512:576] = jnp.where(
        (iota((192, 64), 1) >> 3) == (iota((192, 64), 0) & 7), lin, 0.0
    ).astype(BF16)


def derivative_rows(d_ref, rows, dperm):
    zero = jnp.zeros((8, 216), F32)
    for pair in range(PAIRS):
        parts = []
        for g in (2 * pair, 2 * pair + 1):
            for d in range(3):
                parts.append(d_ref[d, g].astype(F32) if g < 27 else zero)
        rows[pair * 48 : pair * 48 + 48, :] = jnp.concatenate(parts, axis=0).astype(BF16)
    eye = onehot(iota((216, 216), 0) == iota((216, 216), 1))
    dperm[...] = lax.dot_general(
        eye, rows[...], (((1,), (1,)), ((), ())), preferred_element_type=F32
    ).astype(BF16)


def volume_pairs(first, last, s_ref, a_ref, wv, prod, trans):
    def step(pair, carry):
        for half in range(2):
            for t in range(3):
                lanes = slice((half * 3 + t) * 128, (half * 3 + t) * 128 + 128)
                linear = []
                for q8 in range(8):
                    q = jnp.minimum(pair * 16 + half * 8 + q8, 215)
                    s = s_ref[q, t].astype(F32)
                    a = a_ref[q, t].astype(F32)
                    p = (a[:, None, :] * s[None, :, :]).reshape(64, 128)
                    prod[q8 * 64 : q8 * 64 + 64, lanes] = p.astype(BF16)
                    linear.append(a)
                prod[512:576, lanes] = jnp.concatenate(linear, axis=0).astype(BF16)
        out = jnp.dot(wv[...], prod[...], preferred_element_type=F32)
        rows = pl.ds(pl.multiple_of(pair * 48, 48), 48)
        for b in range(8):
            block = jnp.concatenate(
                [out[b * 24 : b * 24 + 24, 0:384], out[b * 24 : b * 24 + 24, 384:768]], axis=0
            ).astype(BF16)
            trans[rows, b * 384 : b * 384 + 384] = block
        return carry

    lax.fori_loop(first, last, step, 0)


def volume_product(dperm, trans, v_ref):
    for chunk in range(8):
        lanes = slice(chunk * 384, chunk * 384 + 384)
        out = jnp.dot(dperm[...], trans[:, lanes], preferred_element_type=F32)
        for t in range(3):
            v_ref[t, chunk * 216 : chunk * 216 + 216, :] = out[:, t * 128 : t * 128 + 128]


def zonal_matrix(kernel_ref, ring, y, z, c, chosen):
    ring[...] = jnp.zeros_like(ring)
    ring[:, 0:192] = jnp.broadcast_to(kernel_ref[...], (8, 192))
    twice = ring[...] + pltpu.roll(ring[...], 192, 1)
    full = jnp.broadcast_to(twice[0:1, :], (192, 384))
    circ = pltpu.roll(full, 0, 1, stride=1, stride_axis=0)[:, 0:192]
    row = iota((64, 192), 0)
    lon = iota((64, 192), 1)
    zr = (z + (row >> 3)) & 7
    ir = row & 7
    wanted = 48 * y + 6 * zr + 3 * c + ir
    pick = ((ir < 3) & (lon == wanted)).astype(F32)
    half = lax.dot_general(
        pick, circ, (((1,), (1,)), ((), ())), precision=HIGH, preferred_element_type=F32
    )
    col = iota((192, 512), 1)
    src = iota((192, 512), 0)
    w = ((2 * y + c) - (col >> 6)) & 7
    zc = (z - ((col >> 3) & 7)) & 7
    ic = col & 7
    wanted = 48 * (w >> 1) + 6 * zc + 3 * (w & 1) + ic
    place = ((ic < 3) & (src == wanted)).astype(F32)
    chosen[...] = jnp.dot(half, place, precision=HIGH, preferred_element_type=F32)


def exchange_kernel(
    s_ref, a_ref, d_ref, jac_ref, off_ref, kernel_ref, numbers_ref,
    own, rem, zon_ref, v_ref,
    rw, re, rs, rn, swaps, wv, rows, dperm, prod, trans, ring, chosen, msend, gath, zout, zrecv,
    send_h, recv_h, send_1, recv_1, send_2, recv_2, send_3, recv_3,
):
    lon = lax.axis_index("lon")
    lat = lax.axis_index("lat")
    y = lon // 16
    z = (lon // 2) % 8
    c = lon % 2
    w = 2 * y + c

    def lon_of(y, z, c):
        return (y * 8 + z) * 2 + c

    along_z = [lon_of(y, (z + o) % 8, c) for o in range(1, 8)]
    around = []
    for o in range(1, 8):
        other = (w + o) % 8
        around.append(lon_of(other // 2, z, other % 2))
    west, east = (lon + 63) % 64, (lon + 1) % 64
    south, north = (lat + 7) % 8, (lat + 1) % 8

    barrier = pltpu.get_barrier_semaphore()
    for target in along_z + around + [west, east]:
        pl.semaphore_signal(barrier, inc=1, device_id={"lon": target}, device_id_type=MESH)
    for target in (south, north):
        pl.semaphore_signal(barrier, inc=1, device_id={"lat": target}, device_id_type=MESH)

    msend[...] = jnp.zeros_like(msend)
    for t in range(3):
        def add(q, total):
            for r in range(8):
                total = total + a_ref[q * 8 + r, t].astype(F32)
            return total

        total = lax.fori_loop(0, 27, add, jnp.zeros((8, 128), F32))
        msend[pl.ds(t, 8, stride=8), :] = total / 216.0
    fill_swaps(numbers_ref, swaps)
    select_own(s_ref, a_ref, swaps, own)

    pl.semaphore_wait(barrier, 18)

    hops = []
    for o in range(1, 8):
        start = pl.multiple_of(((z + o) % 8) * 8, 8)
        hops.append(
            pltpu.make_async_remote_copy(
                src_ref=msend.at[pl.ds(start, 8)],
                dst_ref=gath.at[0, o * 8 : o * 8 + 8],
                send_sem=send_1.at[o],
                recv_sem=recv_1.at[o],
                device_id={"lon": along_z[o - 1]},
                device_id_type=MESH,
            )
        )
    for hop in hops:
        hop.start()
    halos = []
    for index, (src, dst, where) in enumerate(
        [
            (own.at[3], rs, {"lat": north}),
            (own.at[2], rn, {"lat": south}),
            (own.at[1, 2], rw, {"lon": east}),
            (own.at[0, 0], re, {"lon": west}),
        ]
    ):
        halos.append(
            pltpu.make_async_remote_copy(
                src_ref=src, dst_ref=dst, send_sem=send_h.at[index], recv_sem=recv_h.at[index],
                device_id=where, device_id_type=MESH,
            )
        )
    for halo in halos:
        halo.start()

    gath[0, 0:8] = msend[pl.ds(pl.multiple_of(z * 8, 8), 8), :]
    volume_weights(jac_ref, off_ref, wv)
    derivative_rows(d_ref, rows, dperm)
    for hop in hops:
        hop.wait_recv()
    spread = [
        pltpu.make_async_remote_copy(
            src_ref=gath.at[0], dst_ref=gath.at[o], send_sem=send_2.at[o], recv_sem=recv_2.at[o],
            device_id={"lon": around[o - 1]}, device_id_type=MESH,
        )
        for o in range(1, 8)
    ]
    for hop in spread:
        hop.start()
    zonal_matrix(kernel_ref, ring, y, z, c, chosen)
    volume_pairs(0, 5, s_ref, a_ref, wv, prod, trans)
    for hop in spread:
        hop.wait_recv()
    zout[...] = jnp.dot(
        chosen[...], gath[...].reshape(512, 128), precision=HIGH, preferred_element_type=F32
    )
    back = [
        pltpu.make_async_remote_copy(
            src_ref=zout.at[o * 8 : o * 8 + 8], dst_ref=zrecv.at[pl.ds(pl.multiple_of(z * 8, 8), 8)],
            send_sem=send_3.at[o], recv_sem=recv_3.at[o],
            device_id={"lon": along_z[o - 1]}, device_id_type=MESH,
        )
        for o in range(1, 8)
    ]
    for hop in back:
        hop.start()
    zrecv[pl.ds(pl.multiple_of(z * 8, 8), 8), :] = zout[0:8, :]
    volume_pairs(5, PAIRS, s_ref, a_ref, wv, prod, trans)
    volume_product(dperm, trans, v_ref)

    lane = iota((16, 128), 1)
    radial = lane & 63
    for t in range(3):
        def inside(m, carry):
            up = jnp.where(radial == 0, 0.0, pltpu.roll(own[5, t, m].astype(F32), 1, 1))
            down = jnp.where(radial == 63, 0.0, pltpu.roll(own[4, t, m].astype(F32), 127, 1))
            rem[4, t, m] = up.astype(BF16)
            rem[5, t, m] = down.astype(BF16)
            if t > 0:
                rem[0, t, m] = own[1, t - 1, m]
            if t < 2:
                rem[1, t, m] = own[0, t + 1, m]
            return carry

        lax.fori_loop(0, 36, inside, 0)
    for halo in halos:
        halo.wait_recv()
    from_south = jnp.where(lat > 0, 1.0, 0.0).astype(F32)
    from_north = jnp.where(lat < 7, 1.0, 0.0).astype(F32)
    upper = lane >= 64
    for t in range(3):
        def outside(m, carry):
            low = jnp.where(upper, rs[t, m].astype(F32) * from_south, own[3, t, m].astype(F32))
            high = jnp.where(upper, own[2, t, m].astype(F32), rn[t, m].astype(F32) * from_north)
            rem[2, t, m] = pltpu.roll(low, 64, 1).astype(BF16)
            rem[3, t, m] = pltpu.roll(high, 64, 1).astype(BF16)
            if t == 0:
                rem[0, t, m] = rw[m]
            if t == 2:
                rem[1, t, m] = re[m]
            return carry

        lax.fori_loop(0, 36, outside, 0)
    for hop in back:
        hop.wait_recv()
    for t in range(3):
        zon_ref[t] = zrecv[pl.ds(t, 8, stride=8), :]
    for copy in hops + halos + spread + back:
        copy.wait_send()


def exchange(state, adjoint, derivative, jac, off, kernel, numbers):
    vmem = pl.BlockSpec(memory_space=pltpu.VMEM)
    return pl.pallas_call(
        exchange_kernel,
        out_shape=[
            jax.ShapeDtypeStruct((6, 3, 36, 16, 128), BF16),
            jax.ShapeDtypeStruct((6, 3, 36, 16, 128), BF16),
            jax.ShapeDtypeStruct((3, 8, 128), F32),
            jax.ShapeDtypeStruct((3, 1728, 128), F32),
        ],
        in_specs=[vmem] * 7,
        out_specs=[vmem] * 4,
        scratch_shapes=[
            pltpu.VMEM((36, 16, 128), BF16),
            pltpu.VMEM((36, 16, 128), BF16),
            pltpu.VMEM((3, 36, 16, 128), BF16),
            pltpu.VMEM((3, 36, 16, 128), BF16),
            pltpu.VMEM((3, 12, 8, 128), jnp.int32),
            pltpu.VMEM((192, 576), BF16),
            pltpu.VMEM((48 * PAIRS, 216), BF16),
            pltpu.VMEM((216, 48 * PAIRS), BF16),
            pltpu.VMEM((576, 768), BF16),
            pltpu.VMEM((48 * PAIRS, 3072), BF16),
            pltpu.VMEM((8, 384), F32),
            pltpu.VMEM((64, 512), F32),
            pltpu.VMEM((64, 128), F32),
            pltpu.VMEM((8, 64, 128), F32),
            pltpu.VMEM((64, 128), F32),
            pltpu.VMEM((64, 128), F32),
            pltpu.SemaphoreType.DMA((4,)),
            pltpu.SemaphoreType.DMA((4,)),
            pltpu.SemaphoreType.DMA((8,)),
            pltpu.SemaphoreType.DMA((8,)),
            pltpu.SemaphoreType.DMA((8,)),
            pltpu.SemaphoreType.DMA((8,)),
            pltpu.SemaphoreType.DMA((8,)),
            pltpu.SemaphoreType.DMA((8,)),
        ],
        compiler_params=pltpu.CompilerParams(
            collective_id=0, has_side_effects=True, vmem_limit_bytes=VMEM_LIMIT
        ),
    )(state, adjoint, derivative, jac, off, kernel, numbers)


def face_weights(jac_ref, off_ref, wf):
    x = jnp.dot(
        jac_ref[...], onehot((iota((8, 64), 1) & 7) == iota((8, 64), 0)), preferred_element_type=F32
    )
    row = iota((192, 64), 0)
    col = iota((192, 64), 1)
    x = jnp.where((col >> 3) == ((row >> 3) & 7), x, 0.0).astype(BF16)
    r = iota((24, 192), 0)
    k = iota((24, 192), 1)
    y = jnp.dot(
        onehot(((k >> 6) == (r >> 3)) & ((k & 7) == (r & 7))), x, preferred_element_type=F32
    )
    gb = onehot((iota((24, 8), 0) & 7) == iota((24, 8), 1))
    z = lax.dot_general(gb, off_ref[...], (((1,), (1,)), ((), ())), preferred_element_type=F32)
    z = jnp.where((iota((24, 24), 1) >> 3) == (iota((24, 24), 0) >> 3), z, 0.0).astype(BF16)
    lin = jnp.dot(
        z, onehot((iota((24, 8), 0) & 7) == iota((24, 8), 1)), preferred_element_type=F32
    )
    for d in range(3):
        wf[d, :, 0:64] = y[d * 8 : d * 8 + 8]
        wf[d, :, 64:72] = lin[d * 8 : d * 8 + 8]


def faces_kernel(
    own, rem, zon_ref, v_ref, jac_ref, off_ref, numbers_ref, turn_ref, out_ref, swaps, wf, turned, terms
):
    fill_swaps(numbers_ref, swaps)
    face_weights(jac_ref, off_ref, wf)

    def flux(index, carry):
        g = index // 3
        t = index % 3
        code = jnp.broadcast_to(turn_ref[t, pl.ds(g, 1), :], (16, 128))
        b0 = (code & 1) != 0
        b1 = (code & 2) != 0
        b2 = (code & 4) != 0
        for u in range(6):
            for v in range(u, 6):
                p = rem[g, t, u * 6 + v].astype(F32)
                q = rem[g, t, v * 6 + u].astype(F32)
                turned[u * 6 + v] = jnp.where(b0, q, p)
                turned[v * 6 + u] = jnp.where(b0, p, q)
        for v in range(6):
            for u in range(3):
                p = turned[u * 6 + v]
                q = turned[(5 - u) * 6 + v]
                turned[u * 6 + v] = jnp.where(b1, q, p)
                turned[(5 - u) * 6 + v] = jnp.where(b1, p, q)
        for u in range(6):
            for v in range(3):
                p = turned[u * 6 + v]
                q = turned[u * 6 + 5 - v]
                turned[u * 6 + v] = jnp.where(b2, q, p)
                turned[u * 6 + 5 - v] = jnp.where(b2, p, q)
        sigma = jnp.where(g % 2 == 0, -0.5, 0.5).astype(F32)
        weights = wf[g // 2].astype(BF16)
        for m in range(0, 36, 6):
            inputs, jumps, lefts, rights = [], [], [], []
            for k in range(6):
                left = own[g, t, m + k].astype(F32)
                right = turned[m + k]
                ul, wl, ur, wr = left[0:8], left[8:16], right[0:8], right[8:16]
                w = wl - wr
                prods = (w[:, None, :] * ul[None, :, :]).reshape(64, 128)
                inputs.append(jnp.concatenate([prods, w], axis=0).astype(BF16))
                jumps.append(w)
                lefts.append(ul)
                rights.append(ur)
            applied = jnp.dot(
                weights, jnp.concatenate(inputs, axis=1), preferred_element_type=F32
            )
            for k in range(6):
                ul, ur, w = lefts[k], rights[k], jumps[k]
                sl = 1.0 + jnp.sum(ul * ul, axis=0, keepdims=True)
                sr = 1.0 + jnp.sum(ur * ur, axis=0, keepdims=True)
                jump = jnp.sum((ur - ul) * w, axis=0, keepdims=True)
                inv = lax.rsqrt(sl)
                alpha = 0.25 * (sl * inv + jnp.sqrt(sr))
                terms[t, g, m + k] = (
                    sigma * applied[:, k * 128 : k * 128 + 128]
                    + alpha * w
                    - (0.25 * jump * inv) * ul
                )
        return carry

    lax.fori_loop(0, 18, flux, 0)

    def give_back(index, carry):
        t = index // 6
        u = index % 6
        for v in range(6):
            m = u * 6 + v
            parts = [terms[t, g, m] for g in range(6)]
            for s, (i, j) in enumerate(NETWORK):
                swap = swaps[t, s] != 0
                parts[i], parts[j] = (
                    jnp.where(swap, parts[j], parts[i]),
                    jnp.where(swap, parts[i], parts[j]),
                )
            for face in range(6):
                terms[t, face, m] = parts[face]
        return carry

    lax.fori_loop(0, 18, give_back, 0)

    def total(t, carry):
        zon = zon_ref[t]
        for k in range(6):
            for j in range(6):
                for i in range(6):
                    p = k * 36 + j * 6 + i
                    acc = v_ref[t, pl.ds(p, 8, stride=216), :] + zon
                    if i in (0, 5):
                        acc = acc + terms[t, i // 5, k * 6 + j]
                    if j in (0, 5):
                        acc = acc + terms[t, 2 + j // 5, k * 6 + i]
                    if k in (0, 5):
                        acc = acc + terms[t, 4 + k // 5, j * 6 + i]
                    out_ref[p, t] = acc.astype(BF16)
        return carry

    lax.fori_loop(0, 3, total, 0)


def faces(own, rem, zon, vol, jac, off, numbers, turnings):
    vmem = pl.BlockSpec(memory_space=pltpu.VMEM)
    return pl.pallas_call(
        faces_kernel,
        out_shape=jax.ShapeDtypeStruct((216, 3, 8, 128), BF16),
        in_specs=[vmem] * 8,
        out_specs=vmem,
        scratch_shapes=[
            pltpu.VMEM((3, 12, 8, 128), jnp.int32),
            pltpu.VMEM((3, 8, 72), F32),
            pltpu.VMEM((36, 16, 128), F32),
            pltpu.VMEM((3, 6, 36, 8, 128), F32),
        ],
        compiler_params=pltpu.CompilerParams(vmem_limit_bytes=VMEM_LIMIT),
    )(own, rem, zon, vol, jac, off, numbers, turnings)


def body(state, adjoint, derivative, jac_tensor, jac_offset, zonal_kernel, face_numbers, orientation):
    s = jnp.transpose(state, (0, 2, 1, 3))
    a = jnp.transpose(adjoint, (0, 2, 1, 3))
    d = derivative.reshape(3, 27, 8, 216)
    jac = jac_tensor.reshape(192, 8)
    off = jac_offset.reshape(24, 8)
    kernel = zonal_kernel.reshape(1, 192)
    numbers = jnp.transpose(face_numbers, (0, 2, 1))
    turnings = jnp.transpose(orientation, (0, 2, 1))
    own, rem, zon, vol = exchange(s, a, d, jac, off, kernel, numbers)
    out = faces(own, rem, zon, vol, jac, off, numbers, turnings)
    return jnp.transpose(out, (0, 2, 1, 3))


def solution(mesh):
    in_specs = (
        P(None, None, "lon", "lat"),
        P(None, None, "lon", "lat"),
        P(),
        P(),
        P(),
        P(),
        P("lon", "lat", None),
        P("lon", "lat", None),
    )
    out_specs = P(None, None, "lon", "lat")
    return jax.shard_map(body, mesh=mesh, in_specs=in_specs, out_specs=out_specs, check_vma=False)
```

```python
import functools

import jax
import jax.numpy as jnp
from jax import lax
from jax.experimental import pallas as pl
from jax.experimental.pallas import tpu as pltpu
from jax.sharding import PartitionSpec as P

MESH = pl.DeviceIdType.MESH
F32 = jnp.float32
BF16 = jnp.bfloat16
HIGH = lax.Precision.HIGHEST
STOPS = ((4, 0), (6, 1))
NETWORK = [(0, 5), (1, 3), (2, 4), (1, 2), (3, 4), (0, 3), (2, 5), (0, 1), (2, 3), (4, 5), (1, 2), (3, 4)]
VMEM_LIMIT = 56 * 1024 * 1024


def iota(shape, axis):
    return lax.broadcasted_iota(jnp.int32, shape, axis)


def onehot(condition):
    return condition.astype(F32).astype(BF16)


def fill_swaps(numbers_ref, swaps, wide):
    for t in range(3):
        keys = [jnp.broadcast_to(numbers_ref[t, g : g + 1, :], (8, 128)) for g in range(6)]
        for step, (i, j) in enumerate(NETWORK):
            swap = (keys[i] > keys[j]).astype(F32)
            swaps[t, step] = swap
            wide[t, step] = jnp.concatenate([swap, swap], axis=0).astype(BF16)
            keys[i], keys[j] = jnp.minimum(keys[i], keys[j]), jnp.maximum(keys[i], keys[j])


def face_node(face, u, v):
    if face < 2:
        return u * 36 + v * 6 + 5 * face
    if face < 4:
        return u * 36 + 30 * (face - 2) + v
    return 180 * (face - 4) + u * 6 + v


def select_own(s_ref, a_ref, wide, own):
    half = jnp.full((16, 128), 0.5, BF16)

    def step(index, carry):
        t = index // 6
        u = index % 6
        for v in range(6):
            parts = []
            for face in range(6):
                q = face_node(face, u, v)
                both = [s_ref[q, t].astype(F32), a_ref[q, t].astype(F32)]
                parts.append(jnp.concatenate(both, axis=0).astype(BF16))
            for s in range(len(NETWORK) - 1, -1, -1):
                i, j = NETWORK[s]
                swap = wide[t, s] > half
                parts[i], parts[j] = (
                    jnp.where(swap, parts[j], parts[i]),
                    jnp.where(swap, parts[i], parts[j]),
                )
            for g in range(6):
                own[g, t, u * 6 + v] = parts[g]
        return carry

    lax.fori_loop(0, 18, step, 0)


def weights(jac_ref, off_ref, wv, wf):
    x = jnp.dot(
        jac_ref[...], onehot((iota((8, 64), 1) & 7) == iota((8, 64), 0)), preferred_element_type=F32
    )
    row = iota((192, 64), 0)
    col = iota((192, 64), 1)
    x = jnp.where((col >> 3) == ((row >> 3) & 7), x, 0.0).astype(BF16)
    r = iota((24, 192), 0)
    k = iota((24, 192), 1)
    y = jnp.dot(
        onehot(((k >> 6) == (r >> 3)) & ((k & 7) == (r & 7))), x, preferred_element_type=F32
    )
    gb = onehot((iota((24, 8), 0) & 7) == iota((24, 8), 1))
    z = lax.dot_general(gb, off_ref[...], (((1,), (1,)), ((), ())), preferred_element_type=F32)
    z = jnp.where((iota((24, 24), 1) >> 3) == (iota((24, 24), 0) >> 3), z, 0.0).astype(BF16)
    fold = onehot((iota((24, 8), 0) & 7) == iota((24, 8), 1))
    lin = jnp.dot(z, fold, preferred_element_type=F32)
    sums = ((iota((32, 96), 1) - 64) >> 3 == iota((32, 96), 0) >> 3) & (iota((32, 96), 0) >= 8)
    for d in range(3):
        wf[d] = sums.astype(F32)
        wf[d, 0:8, 0:64] = y[d * 8 : d * 8 + 8]
        wf[d, 0:8, 64:72] = lin[d * 8 : d * 8 + 8]
    row = iota((64, 512), 0)
    col = iota((64, 512), 1)
    wide = jnp.dot(
        y.astype(BF16), onehot((row == (col & 63)) & (col < 448)), preferred_element_type=F32
    ) + jnp.dot(
        lin.astype(BF16),
        onehot((iota((8, 512), 0) == (iota((8, 512), 1) & 7)) & (iota((8, 512), 1) >= 448)),
        preferred_element_type=F32,
    )
    row = iota((8, 512), 0)
    col = iota((8, 512), 1)
    owner = jnp.where(col < 448, col >> 6, (col - 448) >> 3)
    keep = (owner == row) & (row < 7)
    for b in range(8):
        parts = [jnp.where(keep, wide[d * 8 + b : d * 8 + b + 1], 0.0) for d in range(3)]
        wv[b * 24 : b * 24 + 24, :] = jnp.concatenate(parts, axis=0)


def derivative_columns(d_ref, dperm):
    q = iota((216, 256), 0)
    col = iota((216, 256), 1)
    place = onehot((q == 7 * (col >> 3) + (col & 7)) & ((col & 7) < 7))
    for d in range(3):
        dperm[:, d * 256 : d * 256 + 256] = lax.dot_general(
            d_ref[d], place, (((0,), (0,)), ((), ())), preferred_element_type=F32
        ).astype(BF16)


def build_pairs(pair, s_ref, a_ref, prod):
    for half in range(2):
        for t in range(3):
            lanes = slice((half * 3 + t) * 128, (half * 3 + t) * 128 + 128)
            linear = []
            for q7 in range(7):
                q = jnp.minimum(pair * 14 + half * 7 + q7, 215)
                s = s_ref[q, t].astype(F32)
                a = a_ref[q, t].astype(F32)
                p = (a[:, None, :] * s[None, :, :]).reshape(64, 128)
                prod[q7 * 64 : q7 * 64 + 64, lanes] = p.astype(BF16)
                linear.append(a)
            prod[448:512, lanes] = jnp.concatenate(linear + linear[6:], axis=0).astype(BF16)


def contract_pairs(pair, wv, prod, trans):
    out = jnp.dot(wv[...].astype(BF16), prod[...], preferred_element_type=F32)
    for d in range(3):
        rows = pl.ds(pl.multiple_of(pair * 16 + d * 256, 16), 16)
        for b in range(8):
            part = out[b * 24 + d * 8 : b * 24 + d * 8 + 8]
            block = jnp.concatenate([part[:, 0:384], part[:, 384:768]], axis=0)
            trans[rows, b * 384 : b * 384 + 384] = block.astype(BF16)


def volume_steps(first, last, s_ref, a_ref, wv, prod_a, prod_b, trans):
    def step(index, carry):
        contract_pairs(2 * index, wv, prod_a, trans)
        build_pairs(2 * index + 1, s_ref, a_ref, prod_b)
        contract_pairs(2 * index + 1, wv, prod_b, trans)
        build_pairs(2 * index + 2, s_ref, a_ref, prod_a)
        return carry

    lax.fori_loop(first, last, step, 0)


def volume_product(dperm, trans, v_ref):
    for chunk in range(8):
        lanes = slice(chunk * 384, chunk * 384 + 384)
        out = jnp.dot(dperm[...], trans[:, lanes], preferred_element_type=F32)
        for t in range(3):
            v_ref[t, chunk * 216 : chunk * 216 + 216, :] = out[:, t * 128 : t * 128 + 128]


def zonal_matrix(kernel_ref, ring, y, z, c, chosen):
    ring[...] = jnp.zeros_like(ring)
    ring[:, 0:192] = jnp.broadcast_to(kernel_ref[...], (8, 192))
    twice = ring[...] + pltpu.roll(ring[...], 192, 1)
    full = jnp.broadcast_to(twice[0:1, :], (192, 384))
    circ = pltpu.roll(full, 0, 1, stride=1, stride_axis=0)[:, 0:192]
    row = iota((64, 192), 0)
    lon = iota((64, 192), 1)
    zr = (z + (row >> 3)) & 7
    ir = row & 7
    wanted = 48 * y + 6 * zr + 3 * c + ir
    pick = ((ir < 3) & (lon == wanted)).astype(F32)
    half = lax.dot_general(
        pick, circ, (((1,), (1,)), ((), ())), precision=HIGH, preferred_element_type=F32
    )
    eight = iota((8, 192), 1) >> 3
    ow = jnp.zeros_like(eight)
    for o in range(1, 8):
        ow = ow + (eight >= 3 * o).astype(jnp.int32)
    ic = eight - 3 * ow
    w = (2 * y + c - ow) & 7
    zc = (z - (iota((8, 192), 1) & 7)) & 7
    wanted = 48 * (w >> 1) + 6 * zc + 3 * (w & 1) + ic
    place = (iota((192, 192), 0) == wanted[0:1, :]).astype(F32)
    chosen[...] = jnp.dot(half, place, precision=HIGH, preferred_element_type=F32)


def flux(g, t, remote, own, turn_ref, wf, terms):
    code = jnp.broadcast_to(turn_ref[t, pl.ds(g, 1), :], (8, 128))
    half = jnp.full((16, 128), 0.5, BF16)
    bits = []
    for bit in (1, 2, 4):
        b = ((code & bit) != 0).astype(F32)
        bits.append(jnp.concatenate([b, b], axis=0).astype(BF16) > half)
    sigma = jnp.where(g % 2 == 0, -0.5, 0.5).astype(F32)
    matrix = wf[g // 2].astype(BF16)

    def swapped(tiles, mask, turn):
        return {n: jnp.where(mask, tiles[turn(n)], tiles[n]) for n in tiles}

    for orbits in (((0, 1),), ((0, 2),), ((1, 2),), ((0, 0), (1, 1), (2, 2))):
        inputs, jumps, lefts = [], [], []
        nodes = []
        for a, b in orbits:
            tiles = {}
            for u in (a, 5 - a):
                for v in (b, 5 - b):
                    tiles[u, v] = remote(t, u * 6 + v)
                    if (v, u) not in tiles:
                        tiles[v, u] = remote(t, v * 6 + u)
            tiles = swapped(tiles, bits[0], lambda n: (n[1], n[0]))
            tiles = swapped(tiles, bits[1], lambda n: (5 - n[0], n[1]))
            tiles = swapped(tiles, bits[2], lambda n: (n[0], 5 - n[1]))
            for n in tiles:
                m = n[0] * 6 + n[1]
                left = own[g, t, m].astype(F32)
                right = tiles[n].astype(F32)
                ul, wl, ur, wr = left[0:8], left[8:16], right[0:8], right[8:16]
                w = wl - wr
                prods = (w[:, None, :] * ul[None, :, :]).reshape(64, 128)
                rows = [prods, w, ul * ul, ur * ur, (ur - ul) * w]
                inputs.append(jnp.concatenate(rows, axis=0).astype(BF16))
                jumps.append(w)
                lefts.append(ul)
                nodes.append(m)
        summed = jnp.dot(matrix, jnp.concatenate(inputs, axis=1), preferred_element_type=F32)
        for k, m in enumerate(nodes):
            lanes = slice(k * 128, k * 128 + 128)
            sl = 1.0 + summed[8:16, lanes]
            sr = 1.0 + summed[16:24, lanes]
            inv = lax.rsqrt(sl)
            alpha = 0.25 * (sl * inv + jnp.sqrt(sr))
            terms[t, g, m] = (
                sigma * summed[0:8, lanes]
                + alpha * jumps[k]
                - (0.25 * summed[24:32, lanes] * inv) * lefts[k]
            )


def finish(swaps, terms, zon, v_ref, out_ref):
    def give_back(index, carry):
        t = index // 6
        u = index % 6
        for v in range(6):
            m = u * 6 + v
            parts = [terms[t, g, m] for g in range(6)]
            for s, (i, j) in enumerate(NETWORK):
                swap = swaps[t, s] > 0.5
                parts[i], parts[j] = (
                    jnp.where(swap, parts[j], parts[i]),
                    jnp.where(swap, parts[i], parts[j]),
                )
            for face in range(6):
                terms[t, face, m] = parts[face]
        return carry

    lax.fori_loop(0, 18, give_back, 0)

    def total(t, carry):
        zon_t = zon[pl.ds(t, 8, stride=8), :]
        for k in range(6):
            for j in range(6):
                for i in range(6):
                    p = k * 36 + j * 6 + i
                    acc = v_ref[t, pl.ds(p, 8, stride=216), :] + zon_t
                    if i in (0, 5):
                        acc = acc + terms[t, i // 5, k * 6 + j]
                    if j in (0, 5):
                        acc = acc + terms[t, 2 + j // 5, k * 6 + i]
                    if k in (0, 5):
                        acc = acc + terms[t, 4 + k // 5, j * 6 + i]
                    out_ref[p, t] = acc.astype(BF16)
        return carry

    lax.fori_loop(0, 3, total, 0)


def kernel(
    s_ref, a_ref, d_ref, jac_ref, off_ref, kernel_ref, numbers_ref, turn_ref, out_ref,
    own, v_ref, rlon, rs, rn, swaps, wide, wv, wf, dperm, prod_a, prod_b, trans,
    ring, chosen, msend, mgot, gath, zout, zrecv, terms,
    send_h, recv_h, send_1, recv_1, send_2, recv_2, send_3, recv_3,
):
    lon = lax.axis_index("lon")
    lat = lax.axis_index("lat")
    y = lon // 16
    z = (lon // 2) % 8
    c = lon % 2
    w = 2 * y + c

    def lon_of(y, z, c):
        return (y * 8 + z) * 2 + c

    along_z = [lon_of(y, (z + o) % 8, c) for o in range(1, 8)]
    around = []
    for o in range(1, 8):
        other = (w + o) % 8
        around.append(lon_of(other // 2, z, other % 2))
    west, east = (lon + 63) % 64, (lon + 1) % 64
    south, north = (lat + 7) % 8, (lat + 1) % 8

    barrier = pltpu.get_barrier_semaphore()
    for target in along_z + around + [west, east]:
        pl.semaphore_signal(barrier, inc=1, device_id={"lon": target}, device_id_type=MESH)
    for target in (south, north):
        pl.semaphore_signal(barrier, inc=1, device_id={"lat": target}, device_id_type=MESH)

    def copy(src, dst, send, recv, where):
        return pltpu.make_async_remote_copy(
            src_ref=src, dst_ref=dst, send_sem=send, recv_sem=recv, device_id=where, device_id_type=MESH
        )

    def volume(first, last):
        volume_steps(first, last, s_ref, a_ref, wv, prod_a, prod_b, trans)

    msend[...] = jnp.zeros_like(msend)

    def add(q, totals):
        totals = list(totals)
        for r in range(8):
            for t in range(3):
                totals[t] = totals[t] + a_ref[q * 8 + r, t].astype(F32)
        return tuple(totals)

    totals = lax.fori_loop(0, 27, add, (jnp.zeros((8, 128), F32),) * 3)
    for t in range(3):
        msend[pl.ds(t, 8, stride=8), :] = totals[t] / 216.0
    fill_swaps(numbers_ref, swaps, wide)
    select_own(s_ref, a_ref, wide, own)
    weights(jac_ref, off_ref, wv, wf)
    zonal_matrix(kernel_ref, ring, y, z, c, chosen)
    derivative_columns(d_ref, dperm)
    build_pairs(0, s_ref, a_ref, prod_a)
    early = z == 0
    stops = [jnp.where(early, e, n) for e, n in STOPS]
    volume(0, stops[0])
    pl.semaphore_wait(barrier, 18)

    hops = []
    for o in range(1, 8):
        start = pl.multiple_of(((z + o) % 8) * 8, 8)
        hops.append(
            copy(
                msend.at[pl.ds(start, 8)], mgot.at[o * 8 : o * 8 + 8], send_1.at[o], recv_1.at[o],
                {"lon": along_z[o - 1]},
            )
        )
    for hop in hops:
        hop.start()
    halos = [
        copy(own.at[1, 2], rlon.at[0], send_h.at[0], recv_h.at[0], {"lon": east}),
        copy(own.at[0, 0], rlon.at[1], send_h.at[1], recv_h.at[1], {"lon": west}),
        copy(own.at[3], rs, send_h.at[2], recv_h.at[2], {"lat": north}),
        copy(own.at[2], rn, send_h.at[3], recv_h.at[3], {"lat": south}),
    ]
    for halo in halos:
        halo.start()
    mgot[0:8] = msend[pl.ds(pl.multiple_of(z * 8, 8), 8), :]
    volume(stops[0], stops[1])
    for hop in hops:
        hop.wait_recv()
    for i in range(3):
        gath[0, i * 8 : i * 8 + 8] = mgot[pl.ds(i, 8, stride=8), :]
    spread = [
        copy(gath.at[0], gath.at[o], send_2.at[o], recv_2.at[o], {"lon": around[o - 1]})
        for o in range(1, 8)
    ]
    for hop in spread:
        hop.start()
    volume(stops[1], 8)
    volume_product(dperm, trans, v_ref)
    for hop in spread:
        hop.wait_recv()
    zout[...] = jnp.dot(
        chosen[...], gath[...].reshape(192, 128), precision=HIGH, preferred_element_type=F32
    )
    place = pl.ds(pl.multiple_of(z * 8, 8), 8)
    back = [
        copy(
            zout.at[o * 8 : o * 8 + 8], zrecv.at[place], send_3.at[o], recv_3.at[o],
            {"lon": along_z[o - 1]},
        )
        for o in range(1, 8)
    ]
    for hop in back:
        hop.start()
    zrecv[place, :] = zout[0:8, :]

    lane = iota((16, 128), 1)
    zero = jnp.zeros((16, 128), BF16)
    inner = (lane & 63).astype(F32).astype(BF16)
    below_first = inner < jnp.full((16, 128), 0.5, BF16)
    above_last = inner > jnp.full((16, 128), 62.5, BF16)
    upper = lane.astype(F32).astype(BF16) > jnp.full((16, 128), 63.5, BF16)

    def faces(g, t, remote):
        flux(g, t, remote, own, turn_ref, wf, terms)

    def from_below(t, m):
        return jnp.where(below_first, zero, pltpu.roll(own[5, t, m], 1, 1))

    def from_above(t, m):
        return jnp.where(above_last, zero, pltpu.roll(own[4, t, m], 127, 1))

    def radial(t, carry):
        faces(4, t, from_below)
        faces(5, t, from_above)
        return carry

    lax.fori_loop(0, 3, radial, 0)

    def inner_lon(index, carry):
        g = index // 2
        faces(g, index % 2 + 1 - g, lambda t, m: own[1 - g, t - 1 + 2 * g, m])
        return carry

    lax.fori_loop(0, 4, inner_lon, 0)
    halos[0].wait_recv()
    halos[1].wait_recv()

    def outer_lon(g, carry):
        faces(g, 2 * g, lambda t, m: rlon[g, m])
        return carry

    lax.fori_loop(0, 2, outer_lon, 0)
    halos[2].wait_recv()
    halos[3].wait_recv()
    has_south = jnp.broadcast_to(jnp.where(lat > 0, 1.0, 0.0).astype(F32), (16, 128)).astype(BF16)
    has_north = jnp.broadcast_to(jnp.where(lat < 7, 1.0, 0.0).astype(F32), (16, 128)).astype(BF16)

    def from_south(t, m):
        return pltpu.roll(jnp.where(upper, rs[t, m] * has_south, own[3, t, m]), 64, 1)

    def from_north(t, m):
        return pltpu.roll(jnp.where(upper, own[2, t, m], rn[t, m] * has_north), 64, 1)

    def lats(t, carry):
        faces(2, t, from_south)
        faces(3, t, from_north)
        return carry

    lax.fori_loop(0, 3, lats, 0)
    for hop in back:
        hop.wait_recv()
    finish(swaps, terms, zrecv, v_ref, out_ref)
    for sent in hops + halos + spread + back:
        sent.wait_send()


def whole(*operands):
    vmem = pl.BlockSpec(memory_space=pltpu.VMEM)
    dma = pltpu.SemaphoreType.DMA
    return pl.pallas_call(
        kernel,
        out_shape=jax.ShapeDtypeStruct((216, 3, 8, 128), BF16),
        in_specs=[vmem] * 8,
        out_specs=vmem,
        scratch_shapes=[
            pltpu.VMEM((6, 3, 36, 16, 128), BF16),
            pltpu.VMEM((3, 1728, 128), F32),
            pltpu.VMEM((2, 36, 16, 128), BF16),
            pltpu.VMEM((3, 36, 16, 128), BF16),
            pltpu.VMEM((3, 36, 16, 128), BF16),
            pltpu.VMEM((3, 12, 8, 128), F32),
            pltpu.VMEM((3, 12, 16, 128), BF16),
            pltpu.VMEM((192, 512), F32),
            pltpu.VMEM((3, 32, 96), F32),
            pltpu.VMEM((216, 768), BF16),
            pltpu.VMEM((512, 768), BF16),
            pltpu.VMEM((512, 768), BF16),
            pltpu.VMEM((768, 3072), BF16),
            pltpu.VMEM((8, 384), F32),
            pltpu.VMEM((64, 192), F32),
            pltpu.VMEM((64, 128), F32),
            pltpu.VMEM((64, 128), F32),
            pltpu.VMEM((8, 24, 128), F32),
            pltpu.VMEM((64, 128), F32),
            pltpu.VMEM((64, 128), F32),
            pltpu.VMEM((3, 6, 36, 8, 128), F32),
            dma((4,)), dma((4,)), dma((8,)), dma((8,)), dma((8,)), dma((8,)), dma((8,)), dma((8,)),
        ],
        compiler_params=pltpu.CompilerParams(
            collective_id=0, has_side_effects=True, vmem_limit_bytes=VMEM_LIMIT
        ),
    )(*operands)


def body(state, adjoint, derivative, jac_tensor, jac_offset, zonal_kernel, face_numbers, orientation):
    s = jnp.transpose(state, (0, 2, 1, 3))
    a = jnp.transpose(adjoint, (0, 2, 1, 3))
    jac = jac_tensor.reshape(192, 8)
    off = jac_offset.reshape(24, 8)
    ring = zonal_kernel.reshape(1, 192)
    numbers = jnp.transpose(face_numbers, (0, 2, 1))
    turnings = jnp.transpose(orientation, (0, 2, 1))
    out = whole(s, a, derivative, jac, off, ring, numbers, turnings)
    return jnp.transpose(out, (0, 2, 1, 3))


def solution(mesh):
    in_specs = (
        P(None, None, "lon", "lat"),
        P(None, None, "lon", "lat"),
        P(),
        P(),
        P(),
        P(),
        P("lon", "lat", None),
        P("lon", "lat", None),
    )
    out_specs = P(None, None, "lon", "lat")
    return jax.shard_map(body, mesh=mesh, in_specs=in_specs, out_specs=out_specs, check_vma=False)
```

```python
import functools

import jax
import jax.numpy as jnp
from jax import lax
from jax.experimental import pallas as pl
from jax.experimental.pallas import tpu as pltpu
from jax.sharding import PartitionSpec as P

MESH = pl.DeviceIdType.MESH
F32 = jnp.float32
BF16 = jnp.bfloat16
HIGH = lax.Precision.HIGHEST
STOPS = ((1, 0), (6, 1), (8, 5))
NETWORK = [(0, 5), (1, 3), (2, 4), (1, 2), (3, 4), (0, 3), (2, 5), (0, 1), (2, 3), (4, 5), (1, 2), (3, 4)]
VMEM_LIMIT = 56 * 1024 * 1024


def iota(shape, axis):
    return lax.broadcasted_iota(jnp.int32, shape, axis)


def onehot(condition):
    return condition.astype(F32).astype(BF16)


def fill_swaps(numbers_ref, swaps, wide):
    for t in range(3):
        keys = [jnp.broadcast_to(numbers_ref[t, g : g + 1, :], (8, 128)) for g in range(6)]
        for step, (i, j) in enumerate(NETWORK):
            swap = (keys[i] > keys[j]).astype(F32)
            swaps[t, step] = swap
            wide[t, step] = jnp.concatenate([swap, swap], axis=0).astype(BF16)
            keys[i], keys[j] = jnp.minimum(keys[i], keys[j]), jnp.maximum(keys[i], keys[j])


def face_node(face, u, v):
    if face < 2:
        return u * 36 + v * 6 + 5 * face
    if face < 4:
        return u * 36 + 30 * (face - 2) + v
    return 180 * (face - 4) + u * 6 + v


def select_own(s_ref, a_ref, wide, own):
    half = jnp.full((16, 128), 0.5, BF16)

    def step(index, carry):
        t = index // 6
        u = index % 6
        for v in range(6):
            parts = []
            for face in range(6):
                q = face_node(face, u, v)
                both = [s_ref[q, t].astype(F32), a_ref[q, t].astype(F32)]
                parts.append(jnp.concatenate(both, axis=0).astype(BF16))
            for s in range(len(NETWORK) - 1, -1, -1):
                i, j = NETWORK[s]
                swap = wide[t, s] > half
                parts[i], parts[j] = (
                    jnp.where(swap, parts[j], parts[i]),
                    jnp.where(swap, parts[i], parts[j]),
                )
            for g in range(6):
                own[g, t, u * 6 + v] = parts[g]
        return carry

    lax.fori_loop(0, 18, step, 0)


def weights(jac_ref, off_ref, wv, wf):
    x = jnp.dot(
        jac_ref[...], onehot((iota((8, 64), 1) & 7) == iota((8, 64), 0)), preferred_element_type=F32
    )
    row = iota((192, 64), 0)
    col = iota((192, 64), 1)
    x = jnp.where((col >> 3) == ((row >> 3) & 7), x, 0.0).astype(BF16)
    r = iota((24, 192), 0)
    k = iota((24, 192), 1)
    y = jnp.dot(
        onehot(((k >> 6) == (r >> 3)) & ((k & 7) == (r & 7))), x, preferred_element_type=F32
    )
    gb = onehot((iota((24, 8), 0) & 7) == iota((24, 8), 1))
    z = lax.dot_general(gb, off_ref[...], (((1,), (1,)), ((), ())), preferred_element_type=F32)
    z = jnp.where((iota((24, 24), 1) >> 3) == (iota((24, 24), 0) >> 3), z, 0.0).astype(BF16)
    fold = onehot((iota((24, 8), 0) & 7) == iota((24, 8), 1))
    lin = jnp.dot(z, fold, preferred_element_type=F32)
    sums = ((iota((32, 96), 1) - 64) >> 3 == iota((32, 96), 0) >> 3) & (iota((32, 96), 0) >= 8)
    for d in range(3):
        wf[d] = sums.astype(F32)
        wf[d, 0:8, 0:64] = y[d * 8 : d * 8 + 8]
        wf[d, 0:8, 64:72] = lin[d * 8 : d * 8 + 8]
    row = iota((64, 512), 0)
    col = iota((64, 512), 1)
    wide = jnp.dot(
        y.astype(BF16), onehot((row == (col & 63)) & (col < 448)), preferred_element_type=F32
    ) + jnp.dot(
        lin.astype(BF16),
        onehot((iota((8, 512), 0) == (iota((8, 512), 1) & 7)) & (iota((8, 512), 1) >= 448)),
        preferred_element_type=F32,
    )
    row = iota((8, 512), 0)
    col = iota((8, 512), 1)
    owner = jnp.where(col < 448, col >> 6, (col - 448) >> 3)
    keep = (owner == row) & (row < 7)
    for b in range(8):
        parts = [jnp.where(keep, wide[d * 8 + b : d * 8 + b + 1], 0.0) for d in range(3)]
        wv[b * 24 : b * 24 + 24, :] = jnp.concatenate(parts, axis=0)


def derivative_columns(d_ref, dperm):
    q = iota((216, 256), 0)
    col = iota((216, 256), 1)
    place = onehot((q == 7 * (col >> 3) + (col & 7)) & ((col & 7) < 7))
    for d in range(3):
        dperm[:, d * 256 : d * 256 + 256] = lax.dot_general(
            d_ref[d], place, (((0,), (0,)), ((), ())), preferred_element_type=F32
        ).astype(BF16)


def build_pairs(pair, s_ref, a_ref, prod):
    for half in range(2):
        for t in range(3):
            lanes = slice((half * 3 + t) * 128, (half * 3 + t) * 128 + 128)
            linear = []
            for q7 in range(7):
                q = jnp.minimum(pair * 14 + half * 7 + q7, 215)
                s = s_ref[q, t].astype(F32)
                a = a_ref[q, t].astype(F32)
                p = (a[:, None, :] * s[None, :, :]).reshape(64, 128)
                prod[q7 * 64 : q7 * 64 + 64, lanes] = p.astype(BF16)
                linear.append(a)
            prod[448:512, lanes] = jnp.concatenate(linear + linear[6:], axis=0).astype(BF16)


def contract_pairs(pair, wv, prod, trans):
    out = jnp.dot(wv[...].astype(BF16), prod[...], preferred_element_type=F32)
    for d in range(3):
        rows = pl.ds(pl.multiple_of(pair * 16 + d * 256, 16), 16)
        for b in range(8):
            part = out[b * 24 + d * 8 : b * 24 + d * 8 + 8]
            block = jnp.concatenate([part[:, 0:384], part[:, 384:768]], axis=0)
            trans[rows, b * 384 : b * 384 + 384] = block.astype(BF16)


def volume_steps(first, last, s_ref, a_ref, wv, prod_a, prod_b, trans):
    def step(index, carry):
        contract_pairs(2 * index, wv, prod_a, trans)
        build_pairs(2 * index + 1, s_ref, a_ref, prod_b)
        contract_pairs(2 * index + 1, wv, prod_b, trans)
        build_pairs(2 * index + 2, s_ref, a_ref, prod_a)
        return carry

    lax.fori_loop(first, last, step, 0)


def volume_product(dperm, trans, v_ref):
    for chunk in range(8):
        lanes = slice(chunk * 384, chunk * 384 + 384)
        out = jnp.dot(dperm[...], trans[:, lanes], preferred_element_type=F32)
        for t in range(3):
            v_ref[t, chunk * 216 : chunk * 216 + 216, :] = out[:, t * 128 : t * 128 + 128]


def zonal_matrix(kernel_ref, ring, y, z, c, chosen):
    ring[...] = jnp.zeros_like(ring)
    ring[:, 0:192] = jnp.broadcast_to(kernel_ref[...], (8, 192))
    twice = ring[...] + pltpu.roll(ring[...], 192, 1)
    full = jnp.broadcast_to(twice[0:1, :], (192, 384))
    circ = pltpu.roll(full, 0, 1, stride=1, stride_axis=0)[:, 0:192]
    row = iota((64, 192), 0)
    lon = iota((64, 192), 1)
    zr = (z + (row >> 3)) & 7
    ir = row & 7
    wanted = 48 * y + 6 * zr + 3 * c + ir
    pick = ((ir < 3) & (lon == wanted)).astype(F32)
    half = lax.dot_general(
        pick, circ, (((1,), (1,)), ((), ())), precision=HIGH, preferred_element_type=F32
    )
    eight = iota((8, 192), 1) >> 3
    ow = jnp.zeros_like(eight)
    for o in range(1, 8):
        ow = ow + (eight >= 3 * o).astype(jnp.int32)
    ic = eight - 3 * ow
    w = (2 * y + c - ow) & 7
    zc = (z - (iota((8, 192), 1) & 7)) & 7
    wanted = 48 * (w >> 1) + 6 * zc + 3 * (w & 1) + ic
    place = (iota((192, 192), 0) == wanted[0:1, :]).astype(F32)
    chosen[...] = jnp.dot(half, place, precision=HIGH, preferred_element_type=F32)


def flux(g, t, remote, own, turn_ref, wf, terms):
    code = jnp.broadcast_to(turn_ref[t, pl.ds(g, 1), :], (8, 128))
    half = jnp.full((16, 128), 0.5, BF16)
    bits = []
    for bit in (1, 2, 4):
        b = ((code & bit) != 0).astype(F32)
        bits.append(jnp.concatenate([b, b], axis=0).astype(BF16) > half)
    sigma = jnp.where(g % 2 == 0, -0.5, 0.5).astype(F32)
    matrix = wf[g // 2].astype(BF16)

    def swapped(tiles, mask, turn):
        return {n: jnp.where(mask, tiles[turn(n)], tiles[n]) for n in tiles}

    for orbits in (((0, 1),), ((0, 2),), ((1, 2),), ((0, 0), (1, 1), (2, 2))):
        inputs, jumps, lefts = [], [], []
        nodes = []
        for a, b in orbits:
            tiles = {}
            for u in (a, 5 - a):
                for v in (b, 5 - b):
                    tiles[u, v] = remote(t, u * 6 + v)
                    if (v, u) not in tiles:
                        tiles[v, u] = remote(t, v * 6 + u)
            tiles = swapped(tiles, bits[0], lambda n: (n[1], n[0]))
            tiles = swapped(tiles, bits[1], lambda n: (5 - n[0], n[1]))
            tiles = swapped(tiles, bits[2], lambda n: (n[0], 5 - n[1]))
            for n in tiles:
                m = n[0] * 6 + n[1]
                left = own[g, t, m].astype(F32)
                right = tiles[n].astype(F32)
                ul, wl, ur, wr = left[0:8], left[8:16], right[0:8], right[8:16]
                w = wl - wr
                prods = (w[:, None, :] * ul[None, :, :]).reshape(64, 128)
                rows = [prods, w, ul * ul, ur * ur, (ur - ul) * w]
                inputs.append(jnp.concatenate(rows, axis=0).astype(BF16))
                jumps.append(w)
                lefts.append(ul)
                nodes.append(m)
        summed = jnp.dot(matrix, jnp.concatenate(inputs, axis=1), preferred_element_type=F32)
        for k, m in enumerate(nodes):
            lanes = slice(k * 128, k * 128 + 128)
            sl = 1.0 + summed[8:16, lanes]
            sr = 1.0 + summed[16:24, lanes]
            inv = lax.rsqrt(sl)
            alpha = 0.25 * (sl * inv + jnp.sqrt(sr))
            terms[t, g, m] = (
                sigma * summed[0:8, lanes]
                + alpha * jumps[k]
                - (0.25 * summed[24:32, lanes] * inv) * lefts[k]
            )


def finish(swaps, terms, zon, v_ref, out_ref):
    def give_back(index, carry):
        t = index // 6
        u = index % 6
        for v in range(6):
            m = u * 6 + v
            parts = [terms[t, g, m] for g in range(6)]
            for s, (i, j) in enumerate(NETWORK):
                swap = swaps[t, s] > 0.5
                parts[i], parts[j] = (
                    jnp.where(swap, parts[j], parts[i]),
                    jnp.where(swap, parts[i], parts[j]),
                )
            for face in range(6):
                terms[t, face, m] = parts[face]
        return carry

    lax.fori_loop(0, 18, give_back, 0)

    def total(t, carry):
        zon_t = zon[pl.ds(t, 8, stride=8), :]
        for k in range(6):
            for j in range(6):
                for i in range(6):
                    p = k * 36 + j * 6 + i
                    acc = v_ref[t, pl.ds(p, 8, stride=216), :] + zon_t
                    if i in (0, 5):
                        acc = acc + terms[t, i // 5, k * 6 + j]
                    if j in (0, 5):
                        acc = acc + terms[t, 2 + j // 5, k * 6 + i]
                    if k in (0, 5):
                        acc = acc + terms[t, 4 + k // 5, j * 6 + i]
                    out_ref[p, t] = acc.astype(BF16)
        return carry

    lax.fori_loop(0, 3, total, 0)


def kernel(
    s_ref, a_ref, d_ref, jac_ref, off_ref, kernel_ref, numbers_ref, turn_ref, out_ref,
    own, v_ref, rlon, to_north, to_south, rs, rn, swaps, wide, wv, wf, dperm, prod_a, prod_b, trans,
    ring, chosen, msend, mgot, gath, zout, zrecv, terms,
    send_h, recv_h, send_1, recv_1, send_2, recv_2, send_3, recv_3,
):
    lon = lax.axis_index("lon")
    lat = lax.axis_index("lat")
    y = lon // 16
    z = (lon // 2) % 8
    c = lon % 2
    w = 2 * y + c

    def lon_of(y, z, c):
        return (y * 8 + z) * 2 + c

    along_z = [lon_of(y, (z + o) % 8, c) for o in range(1, 8)]
    around = []
    for o in range(1, 8):
        other = (w + o) % 8
        around.append(lon_of(other // 2, z, other % 2))
    west, east = (lon + 63) % 64, (lon + 1) % 64
    south, north = (lat + 7) % 8, (lat + 1) % 8

    barrier = pltpu.get_barrier_semaphore()
    for target in along_z + around + [west, east]:
        pl.semaphore_signal(barrier, inc=1, device_id={"lon": target}, device_id_type=MESH)
    for target in (south, north):
        pl.semaphore_signal(barrier, inc=1, device_id={"lat": target}, device_id_type=MESH)

    def copy(src, dst, send, recv, where):
        return pltpu.make_async_remote_copy(
            src_ref=src, dst_ref=dst, send_sem=send, recv_sem=recv, device_id=where, device_id_type=MESH
        )

    def volume(first, last):
        volume_steps(first, last, s_ref, a_ref, wv, prod_a, prod_b, trans)

    msend[...] = jnp.zeros_like(msend)

    def add(q, totals):
        totals = list(totals)
        for r in range(8):
            for t in range(3):
                totals[t] = totals[t] + a_ref[q * 8 + r, t].astype(F32)
        return tuple(totals)

    totals = lax.fori_loop(0, 27, add, (jnp.zeros((8, 128), F32),) * 3)
    for t in range(3):
        msend[pl.ds(t, 8, stride=8), :] = totals[t] / 216.0
    lane = iota((16, 128), 1)
    zero = jnp.zeros((16, 128), BF16)
    inner = (lane & 63).astype(F32).astype(BF16)
    below_first = inner < jnp.full((16, 128), 0.5, BF16)
    above_last = inner > jnp.full((16, 128), 62.5, BF16)
    upper = lane.astype(F32).astype(BF16) > jnp.full((16, 128), 63.5, BF16)

    fill_swaps(numbers_ref, swaps, wide)
    select_own(s_ref, a_ref, wide, own)

    def pack(index, carry):
        t = index // 3
        for v in range(6):
            m = (index % 3) * 6 + v
            to_north[t, m] = jnp.where(upper, own[3, t, m], pltpu.roll(own[3, t, m + 18], 64, 1))
            to_south[t, m] = jnp.where(upper, pltpu.roll(own[2, t, m + 18], 64, 1), own[2, t, m])
        return carry

    lax.fori_loop(0, 9, pack, 0)
    has_north = lat < 7
    has_south = lat > 0

    def blank(ref):
        def step(m, carry):
            for t in range(3):
                ref[t, m] = zero
            return carry

        lax.fori_loop(0, 18, step, 0)

    @pl.when(lat == 7)
    def _():
        blank(rn)

    @pl.when(lat == 0)
    def _():
        blank(rs)

    def prepare():
        weights(jac_ref, off_ref, wv, wf)
        zonal_matrix(kernel_ref, ring, y, z, c, chosen)
        derivative_columns(d_ref, dperm)
        build_pairs(0, s_ref, a_ref, prod_a)

    early = z == 0
    stops = [jnp.where(early, e, n) for e, n in STOPS]

    @pl.when(early)
    def _():
        prepare()
        volume(0, STOPS[0][0])

    pl.semaphore_wait(barrier, 18)

    hops = []
    for o in range(1, 8):
        start = pl.multiple_of(((z + o) % 8) * 8, 8)
        hops.append(
            copy(
                msend.at[pl.ds(start, 8)], mgot.at[o * 8 : o * 8 + 8], send_1.at[o], recv_1.at[o],
                {"lon": along_z[o - 1]},
            )
        )
    for hop in hops:
        hop.start()
    halos = [
        copy(own.at[1, 2], rlon.at[0], send_h.at[0], recv_h.at[0], {"lon": east}),
        copy(own.at[0, 0], rlon.at[1], send_h.at[1], recv_h.at[1], {"lon": west}),
    ]
    northward = copy(to_north, rs, send_h.at[2], recv_h.at[2], {"lat": north})
    southward = copy(to_south, rn, send_h.at[3], recv_h.at[3], {"lat": south})
    for halo in halos:
        halo.start()

    @pl.when(has_north)
    def _():
        northward.start()

    @pl.when(has_south)
    def _():
        southward.start()

    mgot[0:8] = msend[pl.ds(pl.multiple_of(z * 8, 8), 8), :]

    @pl.when(jnp.logical_not(early))
    def _():
        prepare()

    volume(stops[0], stops[1])
    for hop in hops:
        hop.wait_recv()
    for i in range(3):
        gath[0, i * 8 : i * 8 + 8] = mgot[pl.ds(i, 8, stride=8), :]
    spread = [
        copy(gath.at[0], gath.at[o], send_2.at[o], recv_2.at[o], {"lon": around[o - 1]})
        for o in range(1, 8)
    ]
    for hop in spread:
        hop.start()
    volume(stops[1], stops[2])
    for hop in spread:
        hop.wait_recv()
    zout[...] = jnp.dot(
        chosen[...], gath[...].reshape(192, 128), precision=HIGH, preferred_element_type=F32
    )
    place = pl.ds(pl.multiple_of(z * 8, 8), 8)
    back = [
        copy(
            zout.at[o * 8 : o * 8 + 8], zrecv.at[place], send_3.at[o], recv_3.at[o],
            {"lon": along_z[o - 1]},
        )
        for o in range(1, 8)
    ]
    for hop in back:
        hop.start()
    zrecv[place, :] = zout[0:8, :]
    volume(stops[2], 8)
    volume_product(dperm, trans, v_ref)

    def faces(g, t, remote):
        flux(g, t, remote, own, turn_ref, wf, terms)

    def from_below(t, m):
        return jnp.where(below_first, zero, pltpu.roll(own[5, t, m], 1, 1))

    def from_above(t, m):
        return jnp.where(above_last, zero, pltpu.roll(own[4, t, m], 127, 1))

    def radial(t, carry):
        faces(4, t, from_below)
        faces(5, t, from_above)
        return carry

    lax.fori_loop(0, 3, radial, 0)

    def inner_lon(index, carry):
        g = index // 2
        faces(g, index % 2 + 1 - g, lambda t, m: own[1 - g, t - 1 + 2 * g, m])
        return carry

    lax.fori_loop(0, 4, inner_lon, 0)
    halos[0].wait_recv()
    halos[1].wait_recv()

    def outer_lon(g, carry):
        faces(g, 2 * g, lambda t, m: rlon[g, m])
        return carry

    lax.fori_loop(0, 2, outer_lon, 0)

    @pl.when(has_south)
    def _():
        northward.wait_recv()

    @pl.when(has_north)
    def _():
        southward.wait_recv()

    def from_south(t, m):
        if m < 18:
            return pltpu.roll(jnp.where(upper, rs[t, m], own[3, t, m]), 64, 1)
        return jnp.where(upper, pltpu.roll(own[3, t, m], 64, 1), rs[t, m - 18])

    def from_north(t, m):
        if m < 18:
            return pltpu.roll(jnp.where(upper, own[2, t, m], rn[t, m]), 64, 1)
        return jnp.where(upper, rn[t, m - 18], pltpu.roll(own[2, t, m], 64, 1))

    def lats(t, carry):
        faces(2, t, from_south)
        faces(3, t, from_north)
        return carry

    lax.fori_loop(0, 3, lats, 0)
    for hop in back:
        hop.wait_recv()
    finish(swaps, terms, zrecv, v_ref, out_ref)
    for sent in hops + halos + spread + back:
        sent.wait_send()

    @pl.when(has_north)
    def _():
        northward.wait_send()

    @pl.when(has_south)
    def _():
        southward.wait_send()


def whole(*operands):
    vmem = pl.BlockSpec(memory_space=pltpu.VMEM)
    dma = pltpu.SemaphoreType.DMA
    return pl.pallas_call(
        kernel,
        out_shape=jax.ShapeDtypeStruct((216, 3, 8, 128), BF16),
        in_specs=[vmem] * 8,
        out_specs=vmem,
        scratch_shapes=[
            pltpu.VMEM((6, 3, 36, 16, 128), BF16),
            pltpu.VMEM((3, 1728, 128), F32),
            pltpu.VMEM((2, 36, 16, 128), BF16),
            pltpu.VMEM((3, 18, 16, 128), BF16),
            pltpu.VMEM((3, 18, 16, 128), BF16),
            pltpu.VMEM((3, 18, 16, 128), BF16),
            pltpu.VMEM((3, 18, 16, 128), BF16),
            pltpu.VMEM((3, 12, 8, 128), F32),
            pltpu.VMEM((3, 12, 16, 128), BF16),
            pltpu.VMEM((192, 512), F32),
            pltpu.VMEM((3, 32, 96), F32),
            pltpu.VMEM((216, 768), BF16),
            pltpu.VMEM((512, 768), BF16),
            pltpu.VMEM((512, 768), BF16),
            pltpu.VMEM((768, 3072), BF16),
            pltpu.VMEM((8, 384), F32),
            pltpu.VMEM((64, 192), F32),
            pltpu.VMEM((64, 128), F32),
            pltpu.VMEM((64, 128), F32),
            pltpu.VMEM((8, 24, 128), F32),
            pltpu.VMEM((64, 128), F32),
            pltpu.VMEM((64, 128), F32),
            pltpu.VMEM((3, 6, 36, 8, 128), F32),
            dma((4,)), dma((4,)), dma((8,)), dma((8,)), dma((8,)), dma((8,)), dma((8,)), dma((8,)),
        ],
        compiler_params=pltpu.CompilerParams(
            collective_id=0, has_side_effects=True, vmem_limit_bytes=VMEM_LIMIT
        ),
    )(*operands)


def body(state, adjoint, derivative, jac_tensor, jac_offset, zonal_kernel, face_numbers, orientation):
    s = jnp.transpose(state, (0, 2, 1, 3))
    a = jnp.transpose(adjoint, (0, 2, 1, 3))
    jac = jac_tensor.reshape(192, 8)
    off = jac_offset.reshape(24, 8)
    ring = zonal_kernel.reshape(1, 192)
    numbers = jnp.transpose(face_numbers, (0, 2, 1))
    turnings = jnp.transpose(orientation, (0, 2, 1))
    out = whole(s, a, derivative, jac, off, ring, numbers, turnings)
    return jnp.transpose(out, (0, 2, 1, 3))


def solution(mesh):
    in_specs = (
        P(None, None, "lon", "lat"),
        P(None, None, "lon", "lat"),
        P(),
        P(),
        P(),
        P(),
        P("lon", "lat", None),
        P("lon", "lat", None),
    )
    out_specs = P(None, None, "lon", "lat")
    return jax.shard_map(body, mesh=mesh, in_specs=in_specs, out_specs=out_specs, check_vma=False)
```

```python
import functools

import jax
import jax.numpy as jnp
from jax import lax
from jax.experimental import pallas as pl
from jax.experimental.pallas import tpu as pltpu
from jax.sharding import PartitionSpec as P

MESH = pl.DeviceIdType.MESH
F32 = jnp.float32
BF16 = jnp.bfloat16
HIGH = lax.Precision.HIGHEST
NETWORK = [(0, 5), (1, 3), (2, 4), (1, 2), (3, 4), (0, 3), (2, 5), (0, 1), (2, 3), (4, 5), (1, 2), (3, 4)]
VMEM_LIMIT = 30 * 1024 * 1024
FINISH_LIMIT = 20 * 1024 * 1024


def iota(shape, axis):
    return lax.broadcasted_iota(jnp.int32, shape, axis)


def onehot(condition):
    return condition.astype(F32).astype(BF16)


def fill_swaps(numbers_ref, swaps, wide):
    for t in range(3):
        keys = [jnp.broadcast_to(numbers_ref[t, g : g + 1, :], (8, 128)) for g in range(6)]
        for step, (i, j) in enumerate(NETWORK):
            swap = (keys[i] > keys[j]).astype(F32)
            swaps[t, step] = swap
            wide[t, step] = jnp.concatenate([swap, swap], axis=0).astype(BF16)
            keys[i], keys[j] = jnp.minimum(keys[i], keys[j]), jnp.maximum(keys[i], keys[j])


def face_node(face, u, v):
    if face < 2:
        return u * 36 + v * 6 + 5 * face
    if face < 4:
        return u * 36 + 30 * (face - 2) + v
    return 180 * (face - 4) + u * 6 + v


def select_own(s_ref, a_ref, wide, own):
    half = jnp.full((16, 128), 0.5, BF16)

    def step(index, carry):
        t = index // 6
        u = index % 6
        for v in range(6):
            parts = []
            for face in range(6):
                q = face_node(face, u, v)
                both = [s_ref[q, t].astype(F32), a_ref[q, t].astype(F32)]
                parts.append(jnp.concatenate(both, axis=0).astype(BF16))
            for s in range(len(NETWORK) - 1, -1, -1):
                i, j = NETWORK[s]
                swap = wide[t, s] > half
                parts[i], parts[j] = (
                    jnp.where(swap, parts[j], parts[i]),
                    jnp.where(swap, parts[i], parts[j]),
                )
            for g in range(6):
                own[g, t, u * 6 + v] = parts[g]
        return carry

    lax.fori_loop(0, 18, step, 0)


def weights(jac_ref, off_ref, wv, wf):
    x = jnp.dot(
        jac_ref[...], onehot((iota((8, 64), 1) & 7) == iota((8, 64), 0)), preferred_element_type=F32
    )
    row = iota((192, 64), 0)
    col = iota((192, 64), 1)
    x = jnp.where((col >> 3) == ((row >> 3) & 7), x, 0.0).astype(BF16)
    r = iota((24, 192), 0)
    k = iota((24, 192), 1)
    y = jnp.dot(
        onehot(((k >> 6) == (r >> 3)) & ((k & 7) == (r & 7))), x, preferred_element_type=F32
    )
    gb = onehot((iota((24, 8), 0) & 7) == iota((24, 8), 1))
    z = lax.dot_general(gb, off_ref[...], (((1,), (1,)), ((), ())), preferred_element_type=F32)
    z = jnp.where((iota((24, 24), 1) >> 3) == (iota((24, 24), 0) >> 3), z, 0.0).astype(BF16)
    fold = onehot((iota((24, 8), 0) & 7) == iota((24, 8), 1))
    lin = jnp.dot(z, fold, preferred_element_type=F32)
    sums = ((iota((32, 96), 1) - 64) >> 3 == iota((32, 96), 0) >> 3) & (iota((32, 96), 0) >= 8)
    for d in range(3):
        wf[d] = sums.astype(F32)
        wf[d, 0:8, 0:64] = y[d * 8 : d * 8 + 8]
        wf[d, 0:8, 64:72] = lin[d * 8 : d * 8 + 8]
    row = iota((64, 512), 0)
    col = iota((64, 512), 1)
    wide = jnp.dot(
        y.astype(BF16), onehot((row == (col & 63)) & (col < 448)), preferred_element_type=F32
    ) + jnp.dot(
        lin.astype(BF16),
        onehot((iota((8, 512), 0) == (iota((8, 512), 1) & 7)) & (iota((8, 512), 1) >= 448)),
        preferred_element_type=F32,
    )
    row = iota((8, 512), 0)
    col = iota((8, 512), 1)
    owner = jnp.where(col < 448, col >> 6, (col - 448) >> 3)
    keep = (owner == row) & (row < 7)
    for b in range(8):
        parts = [jnp.where(keep, wide[d * 8 + b : d * 8 + b + 1], 0.0) for d in range(3)]
        wv[b * 24 : b * 24 + 24, :] = jnp.concatenate(parts, axis=0)


def derivative_columns(d_ref, dperm):
    q = iota((216, 256), 0)
    col = iota((216, 256), 1)
    place = onehot((q == 7 * (col >> 3) + (col & 7)) & ((col & 7) < 7))
    for d in range(3):
        dperm[:, d * 256 : d * 256 + 256] = lax.dot_general(
            d_ref[d], place, (((0,), (0,)), ((), ())), preferred_element_type=F32
        ).astype(BF16)


def build_pairs(pair, s_ref, a_ref, prod):
    for half in range(2):
        for t in range(3):
            lanes = slice((half * 3 + t) * 128, (half * 3 + t) * 128 + 128)
            linear = []
            for q7 in range(7):
                q = jnp.minimum(pair * 14 + half * 7 + q7, 215)
                s = s_ref[q, t].astype(F32)
                a = a_ref[q, t].astype(F32)
                p = (a[:, None, :] * s[None, :, :]).reshape(64, 128)
                prod[q7 * 64 : q7 * 64 + 64, lanes] = p.astype(BF16)
                linear.append(a)
            prod[448:512, lanes] = jnp.concatenate(linear + linear[6:], axis=0).astype(BF16)


def contract_pairs(pair, wv, prod, trans):
    out = jnp.dot(wv[...].astype(BF16), prod[...], preferred_element_type=F32)
    for d in range(3):
        rows = pl.ds(pl.multiple_of(pair * 16 + d * 256, 16), 16)
        for b in range(8):
            part = out[b * 24 + d * 8 : b * 24 + d * 8 + 8]
            block = jnp.concatenate([part[:, 0:384], part[:, 384:768]], axis=0)
            trans[rows, b * 384 : b * 384 + 384] = block.astype(BF16)


def volume_steps(first, last, s_ref, a_ref, wv, prod_a, prod_b, trans):
    def step(index, carry):
        contract_pairs(2 * index, wv, prod_a, trans)
        build_pairs(2 * index + 1, s_ref, a_ref, prod_b)
        contract_pairs(2 * index + 1, wv, prod_b, trans)
        build_pairs(2 * index + 2, s_ref, a_ref, prod_a)
        return carry

    lax.fori_loop(first, last, step, 0)


def volume_product(dperm, trans, v_ref):
    for chunk in range(8):
        lanes = slice(chunk * 384, chunk * 384 + 384)
        out = jnp.dot(dperm[...], trans[:, lanes], preferred_element_type=F32)
        for t in range(3):
            v_ref[t, chunk * 216 : chunk * 216 + 216, :] = out[:, t * 128 : t * 128 + 128]


def zonal_matrix(kernel_ref, ring, y, z, c, chosen):
    ring[...] = jnp.zeros_like(ring)
    ring[:, 0:192] = jnp.broadcast_to(kernel_ref[...], (8, 192))
    twice = ring[...] + pltpu.roll(ring[...], 192, 1)
    full = jnp.broadcast_to(twice[0:1, :], (192, 384))
    circ = pltpu.roll(full, 0, 1, stride=1, stride_axis=0)[:, 0:192]
    row = iota((64, 192), 0)
    lon = iota((64, 192), 1)
    zr = (z + (row >> 3)) & 7
    ir = row & 7
    wanted = 48 * y + 6 * zr + 3 * c + ir
    pick = ((ir < 3) & (lon == wanted)).astype(F32)
    half = lax.dot_general(
        pick, circ, (((1,), (1,)), ((), ())), precision=HIGH, preferred_element_type=F32
    )
    eight = iota((8, 192), 1) >> 3
    ow = jnp.zeros_like(eight)
    for o in range(1, 8):
        ow = ow + (eight >= 3 * o).astype(jnp.int32)
    ic = eight - 3 * ow
    w = (2 * y + c - ow) & 7
    zc = (z - (iota((8, 192), 1) & 7)) & 7
    wanted = 48 * (w >> 1) + 6 * zc + 3 * (w & 1) + ic
    place = (iota((192, 192), 0) == wanted[0:1, :]).astype(F32)
    chosen[...] = jnp.dot(half, place, precision=HIGH, preferred_element_type=F32)


def flux(g, t, remote, own, turn_ref, wf, terms):
    code = jnp.broadcast_to(turn_ref[t, pl.ds(g, 1), :], (8, 128))
    half = jnp.full((16, 128), 0.5, BF16)
    bits = []
    for bit in (1, 2, 4):
        b = ((code & bit) != 0).astype(F32)
        bits.append(jnp.concatenate([b, b], axis=0).astype(BF16) > half)
    sigma = jnp.where(g % 2 == 0, -0.5, 0.5).astype(F32)
    matrix = wf[g // 2].astype(BF16)

    def swapped(tiles, mask, turn):
        return {n: jnp.where(mask, tiles[turn(n)], tiles[n]) for n in tiles}

    for orbits in (((0, 1),), ((0, 2),), ((1, 2),), ((0, 0), (1, 1), (2, 2))):
        inputs, jumps, lefts = [], [], []
        nodes = []
        for a, b in orbits:
            tiles = {}
            for u in (a, 5 - a):
                for v in (b, 5 - b):
                    tiles[u, v] = remote(t, u * 6 + v)
                    if (v, u) not in tiles:
                        tiles[v, u] = remote(t, v * 6 + u)
            tiles = swapped(tiles, bits[0], lambda n: (n[1], n[0]))
            tiles = swapped(tiles, bits[1], lambda n: (5 - n[0], n[1]))
            tiles = swapped(tiles, bits[2], lambda n: (n[0], 5 - n[1]))
            for n in tiles:
                m = n[0] * 6 + n[1]
                left = own[g, t, m].astype(F32)
                right = tiles[n].astype(F32)
                ul, wl, ur, wr = left[0:8], left[8:16], right[0:8], right[8:16]
                w = wl - wr
                prods = (w[:, None, :] * ul[None, :, :]).reshape(64, 128)
                rows = [prods, w, ul * ul, ur * ur, (ur - ul) * w]
                inputs.append(jnp.concatenate(rows, axis=0).astype(BF16))
                jumps.append(w)
                lefts.append(ul)
                nodes.append(m)
        summed = jnp.dot(matrix, jnp.concatenate(inputs, axis=1), preferred_element_type=F32)
        for k, m in enumerate(nodes):
            lanes = slice(k * 128, k * 128 + 128)
            sl = 1.0 + summed[8:16, lanes]
            sr = 1.0 + summed[16:24, lanes]
            inv = lax.rsqrt(sl)
            alpha = 0.25 * (sl * inv + jnp.sqrt(sr))
            terms[t, g, m] = (
                sigma * summed[0:8, lanes]
                + alpha * jumps[k]
                - (0.25 * summed[24:32, lanes] * inv) * lefts[k]
            )


def finish(swaps, given, terms, zon, v_ref, out_ref):
    def give_back(index, carry):
        t = index // 6
        u = index % 6
        for v in range(6):
            m = u * 6 + v
            parts = [given[t, g, m] for g in range(6)]
            for s, (i, j) in enumerate(NETWORK):
                swap = swaps[t, s] > 0.5
                parts[i], parts[j] = (
                    jnp.where(swap, parts[j], parts[i]),
                    jnp.where(swap, parts[i], parts[j]),
                )
            for face in range(6):
                terms[t, face, m] = parts[face]
        return carry

    lax.fori_loop(0, 18, give_back, 0)

    def total(t, carry):
        zon_t = zon[pl.ds(t, 8, stride=8), :]
        for k in range(6):
            for j in range(6):
                for i in range(6):
                    p = k * 36 + j * 6 + i
                    acc = v_ref[t, pl.ds(p, 8, stride=216), :] + zon_t
                    if i in (0, 5):
                        acc = acc + terms[t, i // 5, k * 6 + j]
                    if j in (0, 5):
                        acc = acc + terms[t, 2 + j // 5, k * 6 + i]
                    if k in (0, 5):
                        acc = acc + terms[t, 4 + k // 5, j * 6 + i]
                    out_ref[p, t] = acc.astype(BF16)
        return carry

    lax.fori_loop(0, 3, total, 0)


def kernel(
    s_hbm, a_hbm, d_ref, jac_ref, off_ref, kernel_ref, numbers_ref, turn_ref,
    terms, v_ref, zon_ref, swaps,
    s_ref, a_ref, own, rlon, to_north, to_south, rs, rn, wide, wv, wf, dperm, prod_a, prod_b, trans,
    ring, chosen, msend, mgot, gath, zout, zrecv,
    load, send_h, recv_h, send_1, recv_1, send_2, recv_2, send_3, recv_3,
):
    lon = lax.axis_index("lon")
    lat = lax.axis_index("lat")
    y = lon // 16
    z = (lon // 2) % 8
    c = lon % 2
    w = 2 * y + c

    def lon_of(y, z, c):
        return (y * 8 + z) * 2 + c

    along_z = [lon_of(y, (z + o) % 8, c) for o in range(1, 8)]
    around = []
    for o in range(1, 8):
        other = (w + o) % 8
        around.append(lon_of(other // 2, z, other % 2))
    west, east = (lon + 63) % 64, (lon + 1) % 64
    south, north = (lat + 7) % 8, (lat + 1) % 8

    barrier = pltpu.get_barrier_semaphore()
    for target in along_z + around + [west, east]:
        pl.semaphore_signal(barrier, inc=1, device_id={"lon": target}, device_id_type=MESH)
    for target in (south, north):
        pl.semaphore_signal(barrier, inc=1, device_id={"lat": target}, device_id_type=MESH)

    def copy(src, dst, send, recv, where):
        return pltpu.make_async_remote_copy(
            src_ref=src, dst_ref=dst, send_sem=send, recv_sem=recv, device_id=where, device_id_type=MESH
        )

    def volume(first, last):
        volume_steps(first, last, s_ref, a_ref, wv, prod_a, prod_b, trans)

    loads = [
        pltpu.make_async_copy(a_hbm, a_ref, load.at[0]),
        pltpu.make_async_copy(s_hbm, s_ref, load.at[1]),
    ]
    for each in loads:
        each.start()
    zonal_matrix(kernel_ref, ring, y, z, c, chosen)
    derivative_columns(d_ref, dperm)
    fill_swaps(numbers_ref, swaps, wide)
    loads[0].wait()

    msend[...] = jnp.zeros_like(msend)

    def add(q, totals):
        totals = list(totals)
        for r in range(8):
            for t in range(3):
                totals[t] = totals[t] + a_ref[q * 8 + r, t].astype(F32)
        return tuple(totals)

    totals = lax.fori_loop(0, 27, add, (jnp.zeros((8, 128), F32),) * 3)
    for t in range(3):
        msend[pl.ds(t, 8, stride=8), :] = totals[t] / 216.0
    lane = iota((16, 128), 1)
    zero = jnp.zeros((16, 128), BF16)
    inner = (lane & 63).astype(F32).astype(BF16)
    below_first = inner < jnp.full((16, 128), 0.5, BF16)
    above_last = inner > jnp.full((16, 128), 62.5, BF16)
    upper = lane.astype(F32).astype(BF16) > jnp.full((16, 128), 63.5, BF16)

    loads[1].wait()
    select_own(s_ref, a_ref, wide, own)

    def pack(index, carry):
        t = index // 3
        for v in range(6):
            m = (index % 3) * 6 + v
            to_north[t, m] = jnp.where(upper, own[3, t, m], pltpu.roll(own[3, t, m + 18], 64, 1))
            to_south[t, m] = jnp.where(upper, pltpu.roll(own[2, t, m + 18], 64, 1), own[2, t, m])
        return carry

    lax.fori_loop(0, 9, pack, 0)
    has_north = lat < 7
    has_south = lat > 0

    def blank(ref):
        def step(m, carry):
            for t in range(3):
                ref[t, m] = zero
            return carry

        lax.fori_loop(0, 18, step, 0)

    @pl.when(lat == 7)
    def _():
        blank(rn)

    @pl.when(lat == 0)
    def _():
        blank(rs)

    def prepare():
        weights(jac_ref, off_ref, wv, wf)
        build_pairs(0, s_ref, a_ref, prod_a)

    early = z < 4
    stops = [
        jnp.where(early, jnp.where(z == 3, 1, 5 - z), 0),
        jnp.where(early, jnp.where(z < 2, 8, 6), 2),
        jnp.where(early, 8, 6),
    ]

    @pl.when(early)
    def _():
        prepare()
        volume(0, stops[0])

    pl.semaphore_wait(barrier, 18)

    hops = []
    for o in range(1, 8):
        start = pl.multiple_of(((z + o) % 8) * 8, 8)
        hops.append(
            copy(
                msend.at[pl.ds(start, 8)], mgot.at[o * 8 : o * 8 + 8], send_1.at[o], recv_1.at[o],
                {"lon": along_z[o - 1]},
            )
        )
    for hop in hops:
        hop.start()
    halos = [
        copy(own.at[1, 2], rlon.at[0], send_h.at[0], recv_h.at[0], {"lon": east}),
        copy(own.at[0, 0], rlon.at[1], send_h.at[1], recv_h.at[1], {"lon": west}),
    ]
    northward = copy(to_north, rs, send_h.at[2], recv_h.at[2], {"lat": north})
    southward = copy(to_south, rn, send_h.at[3], recv_h.at[3], {"lat": south})
    for halo in halos:
        halo.start()

    @pl.when(has_north)
    def _():
        northward.start()

    @pl.when(has_south)
    def _():
        southward.start()

    mgot[0:8] = msend[pl.ds(pl.multiple_of(z * 8, 8), 8), :]

    @pl.when(jnp.logical_not(early))
    def _():
        prepare()

    volume(stops[0], stops[1])
    for hop in hops:
        hop.wait_recv()
    for i in range(3):
        gath[0, i * 8 : i * 8 + 8] = mgot[pl.ds(i, 8, stride=8), :]
    spread = [
        copy(gath.at[0], gath.at[o], send_2.at[o], recv_2.at[o], {"lon": around[o - 1]})
        for o in range(1, 8)
    ]
    for hop in spread:
        hop.start()
    volume(stops[1], stops[2])

    @pl.when(early)
    def _():
        volume_product(dperm, trans, v_ref)

    for hop in spread:
        hop.wait_recv()
    zout[...] = jnp.dot(
        chosen[...], gath[...].reshape(192, 128), precision=HIGH, preferred_element_type=F32
    )
    place = pl.ds(pl.multiple_of(z * 8, 8), 8)
    back = [
        copy(
            zout.at[o * 8 : o * 8 + 8], zrecv.at[place], send_3.at[o], recv_3.at[o],
            {"lon": along_z[o - 1]},
        )
        for o in range(1, 8)
    ]
    for hop in back:
        hop.start()
    zrecv[place, :] = zout[0:8, :]
    @pl.when(jnp.logical_not(early))
    def _():
        volume(stops[2], 8)
        volume_product(dperm, trans, v_ref)

    def faces(g, t, remote):
        flux(g, t, remote, own, turn_ref, wf, terms)

    def from_below(t, m):
        return jnp.where(below_first, zero, pltpu.roll(own[5, t, m], 1, 1))

    def from_above(t, m):
        return jnp.where(above_last, zero, pltpu.roll(own[4, t, m], 127, 1))

    def radial(t, carry):
        faces(4, t, from_below)
        faces(5, t, from_above)
        return carry

    lax.fori_loop(0, 3, radial, 0)

    def inner_lon(index, carry):
        g = index // 2
        faces(g, index % 2 + 1 - g, lambda t, m: own[1 - g, t - 1 + 2 * g, m])
        return carry

    lax.fori_loop(0, 4, inner_lon, 0)
    halos[0].wait_recv()
    halos[1].wait_recv()

    def outer_lon(g, carry):
        faces(g, 2 * g, lambda t, m: rlon[g, m])
        return carry

    lax.fori_loop(0, 2, outer_lon, 0)

    @pl.when(has_south)
    def _():
        northward.wait_recv()

    @pl.when(has_north)
    def _():
        southward.wait_recv()

    def from_south(t, m):
        if m < 18:
            return pltpu.roll(jnp.where(upper, rs[t, m], own[3, t, m]), 64, 1)
        return jnp.where(upper, pltpu.roll(own[3, t, m], 64, 1), rs[t, m - 18])

    def from_north(t, m):
        if m < 18:
            return pltpu.roll(jnp.where(upper, own[2, t, m], rn[t, m]), 64, 1)
        return jnp.where(upper, rn[t, m - 18], pltpu.roll(own[2, t, m], 64, 1))

    def lats(t, carry):
        faces(2, t, from_south)
        faces(3, t, from_north)
        return carry

    lax.fori_loop(0, 3, lats, 0)
    for hop in back:
        hop.wait_recv()
    zon_ref[...] = zrecv[...]
    for sent in hops + halos + spread + back:
        sent.wait_send()

    @pl.when(has_north)
    def _():
        northward.wait_send()

    @pl.when(has_south)
    def _():
        southward.wait_send()


def exchange(*operands):
    vmem = pl.BlockSpec(memory_space=pltpu.VMEM)
    dma = pltpu.SemaphoreType.DMA
    return pl.pallas_call(
        kernel,
        out_shape=[
            jax.ShapeDtypeStruct((3, 6, 36, 8, 128), F32),
            jax.ShapeDtypeStruct((3, 1728, 128), F32),
            jax.ShapeDtypeStruct((64, 128), F32),
            jax.ShapeDtypeStruct((3, 12, 8, 128), F32),
        ],
        in_specs=[pl.BlockSpec(memory_space=pltpu.HBM)] * 2 + [vmem] * 6,
        out_specs=[vmem] * 4,
        scratch_shapes=[
            pltpu.VMEM((216, 3, 8, 128), BF16),
            pltpu.VMEM((216, 3, 8, 128), BF16),
            pltpu.VMEM((6, 3, 36, 16, 128), BF16),
            pltpu.VMEM((2, 36, 16, 128), BF16),
            pltpu.VMEM((3, 18, 16, 128), BF16),
            pltpu.VMEM((3, 18, 16, 128), BF16),
            pltpu.VMEM((3, 18, 16, 128), BF16),
            pltpu.VMEM((3, 18, 16, 128), BF16),
            pltpu.VMEM((3, 12, 16, 128), BF16),
            pltpu.VMEM((192, 512), F32),
            pltpu.VMEM((3, 32, 96), F32),
            pltpu.VMEM((216, 768), BF16),
            pltpu.VMEM((512, 768), BF16),
            pltpu.VMEM((512, 768), BF16),
            pltpu.VMEM((768, 3072), BF16),
            pltpu.VMEM((8, 384), F32),
            pltpu.VMEM((64, 192), F32),
            pltpu.VMEM((64, 128), F32),
            pltpu.VMEM((64, 128), F32),
            pltpu.VMEM((8, 24, 128), F32),
            pltpu.VMEM((64, 128), F32),
            pltpu.VMEM((64, 128), F32),
            dma((2,)), dma((4,)), dma((4,)), dma((8,)), dma((8,)), dma((8,)), dma((8,)), dma((8,)), dma((8,)),
        ],
        compiler_params=pltpu.CompilerParams(
            collective_id=0, has_side_effects=True, vmem_limit_bytes=VMEM_LIMIT
        ),
    )(*operands)


def finish_kernel(terms_in, v_ref, zon_ref, swaps, out_ref, terms):
    finish(swaps, terms_in, terms, zon_ref, v_ref, out_ref)


def finished(*operands):
    vmem = pl.BlockSpec(memory_space=pltpu.VMEM)
    return pl.pallas_call(
        finish_kernel,
        out_shape=jax.ShapeDtypeStruct((216, 3, 8, 128), BF16),
        in_specs=[vmem] * 4,
        out_specs=vmem,
        scratch_shapes=[pltpu.VMEM((3, 6, 36, 8, 128), F32)],
        compiler_params=pltpu.CompilerParams(vmem_limit_bytes=FINISH_LIMIT),
    )(*operands)


def body(state, adjoint, derivative, jac_tensor, jac_offset, zonal_kernel, face_numbers, orientation):
    s = jnp.transpose(state, (0, 2, 1, 3))
    a = jnp.transpose(adjoint, (0, 2, 1, 3))
    jac = jac_tensor.reshape(192, 8)
    off = jac_offset.reshape(24, 8)
    ring = zonal_kernel.reshape(1, 192)
    numbers = jnp.transpose(face_numbers, (0, 2, 1))
    turnings = jnp.transpose(orientation, (0, 2, 1))
    s, a, derivative, jac, off, ring, numbers, turnings = [
        pltpu.with_memory_space_constraint(x, pltpu.HBM)
        for x in (s, a, derivative, jac, off, ring, numbers, turnings)
    ]
    parts = exchange(s, a, derivative, jac, off, ring, numbers, turnings)
    out = finished(*parts)
    return jnp.transpose(out, (0, 2, 1, 3))


def solution(mesh):
    in_specs = (
        P(None, None, "lon", "lat"),
        P(None, None, "lon", "lat"),
        P(),
        P(),
        P(),
        P(),
        P("lon", "lat", None),
        P("lon", "lat", None),
    )
    out_specs = P(None, None, "lon", "lat")
    return jax.shard_map(body, mesh=mesh, in_specs=in_specs, out_specs=out_specs, check_vma=False)
```

```python
import functools

import jax
import jax.numpy as jnp
from jax import lax
from jax.experimental import pallas as pl
from jax.experimental.pallas import tpu as pltpu
from jax.sharding import PartitionSpec as P

MESH = pl.DeviceIdType.MESH
F32 = jnp.float32
BF16 = jnp.bfloat16
HIGH = lax.Precision.HIGHEST
NETWORK = [(0, 5), (1, 3), (2, 4), (1, 2), (3, 4), (0, 3), (2, 5), (0, 1), (2, 3), (4, 5), (1, 2), (3, 4)]
VMEM_LIMIT = 30 * 1024 * 1024
FINISH_LIMIT = 20 * 1024 * 1024


def iota(shape, axis):
    return lax.broadcasted_iota(jnp.int32, shape, axis)


def onehot(condition):
    return condition.astype(F32).astype(BF16)


def fill_swaps(numbers_ref, swaps, wide):
    for t in range(3):
        keys = [jnp.broadcast_to(numbers_ref[t, g : g + 1, :], (8, 128)) for g in range(6)]
        for step, (i, j) in enumerate(NETWORK):
            swap = (keys[i] > keys[j]).astype(F32)
            swaps[t, step] = swap
            wide[t, step] = jnp.concatenate([swap, swap], axis=0).astype(BF16)
            keys[i], keys[j] = jnp.minimum(keys[i], keys[j]), jnp.maximum(keys[i], keys[j])


def face_node(face, u, v):
    if face < 2:
        return u * 36 + v * 6 + 5 * face
    if face < 4:
        return u * 36 + 30 * (face - 2) + v
    return 180 * (face - 4) + u * 6 + v


def select_own(s_ref, a_ref, wide, own):
    half = jnp.full((16, 128), 0.5, BF16)

    def step(index, carry):
        t = index // 6
        u = index % 6
        for v in range(6):
            parts = []
            for face in range(6):
                q = face_node(face, u, v)
                both = [s_ref[q, t].astype(F32), a_ref[q, t].astype(F32)]
                parts.append(jnp.concatenate(both, axis=0).astype(BF16))
            for s in range(len(NETWORK) - 1, -1, -1):
                i, j = NETWORK[s]
                swap = wide[t, s] > half
                parts[i], parts[j] = (
                    jnp.where(swap, parts[j], parts[i]),
                    jnp.where(swap, parts[i], parts[j]),
                )
            for g in range(6):
                own[g, t, u * 6 + v] = parts[g]
        return carry

    lax.fori_loop(0, 18, step, 0)


def weights(jac_ref, off_ref, wv, wf):
    x = jnp.dot(
        jac_ref[...], onehot((iota((8, 64), 1) & 7) == iota((8, 64), 0)), preferred_element_type=F32
    )
    row = iota((192, 64), 0)
    col = iota((192, 64), 1)
    x = jnp.where((col >> 3) == ((row >> 3) & 7), x, 0.0).astype(BF16)
    r = iota((24, 192), 0)
    k = iota((24, 192), 1)
    y = jnp.dot(
        onehot(((k >> 6) == (r >> 3)) & ((k & 7) == (r & 7))), x, preferred_element_type=F32
    )
    gb = onehot((iota((24, 8), 0) & 7) == iota((24, 8), 1))
    z = lax.dot_general(gb, off_ref[...], (((1,), (1,)), ((), ())), preferred_element_type=F32)
    z = jnp.where((iota((24, 24), 1) >> 3) == (iota((24, 24), 0) >> 3), z, 0.0).astype(BF16)
    fold = onehot((iota((24, 8), 0) & 7) == iota((24, 8), 1))
    lin = jnp.dot(z, fold, preferred_element_type=F32)
    sums = ((iota((32, 96), 1) - 64) >> 3 == iota((32, 96), 0) >> 3) & (iota((32, 96), 0) >= 8)
    for d in range(3):
        wf[d] = sums.astype(F32)
        wf[d, 0:8, 0:64] = y[d * 8 : d * 8 + 8]
        wf[d, 0:8, 64:72] = lin[d * 8 : d * 8 + 8]
    row = iota((64, 512), 0)
    col = iota((64, 512), 1)
    wide = jnp.dot(
        y.astype(BF16), onehot((row == (col & 63)) & (col < 448)), preferred_element_type=F32
    ) + jnp.dot(
        lin.astype(BF16),
        onehot((iota((8, 512), 0) == (iota((8, 512), 1) & 7)) & (iota((8, 512), 1) >= 448)),
        preferred_element_type=F32,
    )
    row = iota((8, 512), 0)
    col = iota((8, 512), 1)
    owner = jnp.where(col < 448, col >> 6, (col - 448) >> 3)
    keep = (owner == row) & (row < 7)
    for b in range(8):
        parts = [jnp.where(keep, wide[d * 8 + b : d * 8 + b + 1], 0.0) for d in range(3)]
        wv[b * 24 : b * 24 + 24, :] = jnp.concatenate(parts, axis=0)


def derivative_columns(d_ref, dperm):
    q = iota((216, 256), 0)
    col = iota((216, 256), 1)
    place = onehot((q == 7 * (col >> 3) + (col & 7)) & ((col & 7) < 7))
    for d in range(3):
        dperm[:, d * 256 : d * 256 + 256] = lax.dot_general(
            d_ref[d], place, (((0,), (0,)), ((), ())), preferred_element_type=F32
        ).astype(BF16)


def build_pairs(pair, s_ref, a_ref, prod):
    for half in range(2):
        for t in range(3):
            lanes = slice((half * 3 + t) * 128, (half * 3 + t) * 128 + 128)
            linear = []
            for q7 in range(7):
                q = jnp.minimum(pair * 14 + half * 7 + q7, 215)
                s = s_ref[q, t].astype(F32)
                a = a_ref[q, t].astype(F32)
                twice = jnp.concatenate([s, s], axis=0).astype(BF16)
                for k in range(4):
                    two = [jnp.broadcast_to(a[r : r + 1], (8, 128)) for r in (2 * k, 2 * k + 1)]
                    row = q7 * 64 + k * 16
                    prod[row : row + 16, lanes] = jnp.concatenate(two, axis=0).astype(BF16) * twice
                linear.append(a)
            prod[448:512, lanes] = jnp.concatenate(linear + linear[6:], axis=0).astype(BF16)


def contract_pairs(pair, wv, prod, trans):
    out = jnp.dot(wv[...].astype(BF16), prod[...], preferred_element_type=F32)
    for d in range(3):
        rows = pl.ds(pl.multiple_of(pair * 16 + d * 256, 16), 16)
        for b in range(8):
            part = out[b * 24 + d * 8 : b * 24 + d * 8 + 8]
            block = jnp.concatenate([part[:, 0:384], part[:, 384:768]], axis=0)
            trans[rows, b * 384 : b * 384 + 384] = block.astype(BF16)


def volume_steps(first, last, s_ref, a_ref, wv, prod_a, prod_b, trans):
    def step(index, carry):
        contract_pairs(2 * index, wv, prod_a, trans)
        build_pairs(2 * index + 1, s_ref, a_ref, prod_b)
        contract_pairs(2 * index + 1, wv, prod_b, trans)
        build_pairs(2 * index + 2, s_ref, a_ref, prod_a)
        return carry

    lax.fori_loop(first, last, step, 0)


def volume_product(dperm, trans, v_ref):
    for chunk in range(8):
        lanes = slice(chunk * 384, chunk * 384 + 384)
        out = jnp.dot(dperm[...], trans[:, lanes], preferred_element_type=F32)
        for t in range(3):
            v_ref[t, chunk * 216 : chunk * 216 + 216, :] = out[:, t * 128 : t * 128 + 128]


def zonal_matrix(kernel_ref, ring, y, z, c, chosen):
    ring[...] = jnp.zeros_like(ring)
    ring[:, 0:192] = jnp.broadcast_to(kernel_ref[...], (8, 192))
    twice = ring[...] + pltpu.roll(ring[...], 192, 1)
    full = jnp.broadcast_to(twice[0:1, :], (192, 384))
    circ = pltpu.roll(full, 0, 1, stride=1, stride_axis=0)[:, 0:192]
    row = iota((64, 192), 0)
    lon = iota((64, 192), 1)
    zr = (z + (row >> 3)) & 7
    ir = row & 7
    wanted = 48 * y + 6 * zr + 3 * c + ir
    pick = ((ir < 3) & (lon == wanted)).astype(F32)
    half = lax.dot_general(
        pick, circ, (((1,), (1,)), ((), ())), precision=HIGH, preferred_element_type=F32
    )
    eight = iota((8, 192), 1) >> 3
    ow = jnp.zeros_like(eight)
    for o in range(1, 8):
        ow = ow + (eight >= 3 * o).astype(jnp.int32)
    ic = eight - 3 * ow
    w = (2 * y + c - ow) & 7
    zc = (z - (iota((8, 192), 1) & 7)) & 7
    wanted = 48 * (w >> 1) + 6 * zc + 3 * (w & 1) + ic
    place = (iota((192, 192), 0) == wanted[0:1, :]).astype(F32)
    chosen[...] = jnp.dot(half, place, precision=HIGH, preferred_element_type=F32)


def flux(g, t, remote, own, turn_ref, wf, terms):
    code = jnp.broadcast_to(turn_ref[t, pl.ds(g, 1), :], (8, 128))
    half = jnp.full((16, 128), 0.5, BF16)
    bits = []
    for bit in (1, 2, 4):
        b = ((code & bit) != 0).astype(F32)
        bits.append(jnp.concatenate([b, b], axis=0).astype(BF16) > half)
    sigma = jnp.where(g % 2 == 0, -0.5, 0.5).astype(F32)
    matrix = wf[g // 2].astype(BF16)

    def swapped(tiles, mask, turn):
        return {n: jnp.where(mask, tiles[turn(n)], tiles[n]) for n in tiles}

    for orbits in (((0, 1),), ((0, 2),), ((1, 2),), ((0, 0), (1, 1), (2, 2))):
        inputs, jumps, lefts = [], [], []
        nodes = []
        for a, b in orbits:
            tiles = {}
            for u in (a, 5 - a):
                for v in (b, 5 - b):
                    tiles[u, v] = remote(t, u * 6 + v)
                    if (v, u) not in tiles:
                        tiles[v, u] = remote(t, v * 6 + u)
            tiles = swapped(tiles, bits[0], lambda n: (n[1], n[0]))
            tiles = swapped(tiles, bits[1], lambda n: (5 - n[0], n[1]))
            tiles = swapped(tiles, bits[2], lambda n: (n[0], 5 - n[1]))
            for n in tiles:
                m = n[0] * 6 + n[1]
                left = own[g, t, m].astype(F32)
                right = tiles[n].astype(F32)
                ul, wl, ur, wr = left[0:8], left[8:16], right[0:8], right[8:16]
                w = wl - wr
                prods = (w[:, None, :] * ul[None, :, :]).reshape(64, 128)
                rows = [prods, w, ul * ul, ur * ur, (ur - ul) * w]
                inputs.append(jnp.concatenate(rows, axis=0).astype(BF16))
                jumps.append(w)
                lefts.append(ul)
                nodes.append(m)
        summed = jnp.dot(matrix, jnp.concatenate(inputs, axis=1), preferred_element_type=F32)
        for k, m in enumerate(nodes):
            lanes = slice(k * 128, k * 128 + 128)
            sl = 1.0 + summed[8:16, lanes]
            sr = 1.0 + summed[16:24, lanes]
            inv = lax.rsqrt(sl)
            alpha = 0.25 * (sl * inv + jnp.sqrt(sr))
            terms[t, g, m] = (
                sigma * summed[0:8, lanes]
                + alpha * jumps[k]
                - (0.25 * summed[24:32, lanes] * inv) * lefts[k]
            )


def finish(swaps, given, terms, zon, v_ref, out_ref):
    def give_back(index, carry):
        t = index // 6
        u = index % 6
        for v in range(6):
            m = u * 6 + v
            parts = [given[t, g, m] for g in range(6)]
            for s, (i, j) in enumerate(NETWORK):
                swap = swaps[t, s] > 0.5
                parts[i], parts[j] = (
                    jnp.where(swap, parts[j], parts[i]),
                    jnp.where(swap, parts[i], parts[j]),
                )
            for face in range(6):
                terms[t, face, m] = parts[face]
        return carry

    lax.fori_loop(0, 18, give_back, 0)

    def total(t, carry):
        zon_t = zon[pl.ds(t, 8, stride=8), :]
        for k in range(6):
            for j in range(6):
                for i in range(6):
                    p = k * 36 + j * 6 + i
                    acc = v_ref[t, pl.ds(p, 8, stride=216), :] + zon_t
                    if i in (0, 5):
                        acc = acc + terms[t, i // 5, k * 6 + j]
                    if j in (0, 5):
                        acc = acc + terms[t, 2 + j // 5, k * 6 + i]
                    if k in (0, 5):
                        acc = acc + terms[t, 4 + k // 5, j * 6 + i]
                    out_ref[p, t] = acc.astype(BF16)
        return carry

    lax.fori_loop(0, 3, total, 0)


def kernel(
    s_hbm, a_hbm, d_ref, jac_ref, off_ref, kernel_ref, numbers_ref, turn_ref,
    terms, v_ref, zon_ref, swaps,
    s_ref, a_ref, own, rlon, to_north, to_south, rs, rn, wide, wv, wf, dperm, prod_a, prod_b, trans,
    ring, chosen, msend, mgot, gath, zout, zrecv,
    load, send_h, recv_h, send_1, recv_1, send_2, recv_2, send_3, recv_3,
):
    lon = lax.axis_index("lon")
    lat = lax.axis_index("lat")
    y = lon // 16
    z = (lon // 2) % 8
    c = lon % 2
    w = 2 * y + c

    def lon_of(y, z, c):
        return (y * 8 + z) * 2 + c

    along_z = [lon_of(y, (z + o) % 8, c) for o in range(1, 8)]
    around = []
    for o in range(1, 8):
        other = (w + o) % 8
        around.append(lon_of(other // 2, z, other % 2))
    west, east = (lon + 63) % 64, (lon + 1) % 64
    south, north = (lat + 7) % 8, (lat + 1) % 8

    barrier = pltpu.get_barrier_semaphore()
    for target in along_z + around + [west, east]:
        pl.semaphore_signal(barrier, inc=1, device_id={"lon": target}, device_id_type=MESH)
    for target in (south, north):
        pl.semaphore_signal(barrier, inc=1, device_id={"lat": target}, device_id_type=MESH)

    def copy(src, dst, send, recv, where):
        return pltpu.make_async_remote_copy(
            src_ref=src, dst_ref=dst, send_sem=send, recv_sem=recv, device_id=where, device_id_type=MESH
        )

    def volume(first, last):
        volume_steps(first, last, s_ref, a_ref, wv, prod_a, prod_b, trans)

    loads = [
        pltpu.make_async_copy(a_hbm, a_ref, load.at[0]),
        pltpu.make_async_copy(s_hbm, s_ref, load.at[1]),
    ]
    for each in loads:
        each.start()
    zonal_matrix(kernel_ref, ring, y, z, c, chosen)
    derivative_columns(d_ref, dperm)
    fill_swaps(numbers_ref, swaps, wide)
    loads[0].wait()

    msend[...] = jnp.zeros_like(msend)

    def add(q, totals):
        totals = list(totals)
        for r in range(8):
            for t in range(3):
                totals[t] = totals[t] + a_ref[q * 8 + r, t].astype(F32)
        return tuple(totals)

    totals = lax.fori_loop(0, 27, add, (jnp.zeros((8, 128), F32),) * 3)
    for t in range(3):
        msend[pl.ds(t, 8, stride=8), :] = totals[t] / 216.0
    lane = iota((16, 128), 1)
    zero = jnp.zeros((16, 128), BF16)
    inner = (lane & 63).astype(F32).astype(BF16)
    below_first = inner < jnp.full((16, 128), 0.5, BF16)
    above_last = inner > jnp.full((16, 128), 62.5, BF16)
    upper = lane.astype(F32).astype(BF16) > jnp.full((16, 128), 63.5, BF16)

    loads[1].wait()
    select_own(s_ref, a_ref, wide, own)

    def pack(index, carry):
        t = index // 3
        for v in range(6):
            m = (index % 3) * 6 + v
            to_north[t, m] = jnp.where(upper, own[3, t, m], pltpu.roll(own[3, t, m + 18], 64, 1))
            to_south[t, m] = jnp.where(upper, pltpu.roll(own[2, t, m + 18], 64, 1), own[2, t, m])
        return carry

    lax.fori_loop(0, 9, pack, 0)
    has_north = lat < 7
    has_south = lat > 0

    def blank(ref):
        def step(m, carry):
            for t in range(3):
                ref[t, m] = zero
            return carry

        lax.fori_loop(0, 18, step, 0)

    @pl.when(lat == 7)
    def _():
        blank(rn)

    @pl.when(lat == 0)
    def _():
        blank(rs)

    def prepare():
        weights(jac_ref, off_ref, wv, wf)
        build_pairs(0, s_ref, a_ref, prod_a)

    early = z < 4
    stops = [
        jnp.where(early, jnp.where(z == 3, 1, 5 - z), 0),
        jnp.where(early, jnp.where(z < 2, 8, 6), 2),
        jnp.where(early, 8, 4),
    ]

    @pl.when(early)
    def _():
        prepare()
        volume(0, stops[0])

    pl.semaphore_wait(barrier, 18)

    hops = []
    for o in range(1, 8):
        start = pl.multiple_of(((z + o) % 8) * 8, 8)
        hops.append(
            copy(
                msend.at[pl.ds(start, 8)], mgot.at[o * 8 : o * 8 + 8], send_1.at[o], recv_1.at[o],
                {"lon": along_z[o - 1]},
            )
        )
    for hop in hops:
        hop.start()
    halos = [
        copy(own.at[1, 2], rlon.at[0], send_h.at[0], recv_h.at[0], {"lon": east}),
        copy(own.at[0, 0], rlon.at[1], send_h.at[1], recv_h.at[1], {"lon": west}),
    ]
    northward = copy(to_north, rs, send_h.at[2], recv_h.at[2], {"lat": north})
    southward = copy(to_south, rn, send_h.at[3], recv_h.at[3], {"lat": south})
    @pl.when(has_north)
    def _():
        northward.start()

    @pl.when(has_south)
    def _():
        southward.start()

    mgot[0:8] = msend[pl.ds(pl.multiple_of(z * 8, 8), 8), :]

    @pl.when(jnp.logical_not(early))
    def _():
        prepare()

    volume(stops[0], stops[1])
    for hop in hops:
        hop.wait_recv()
    for i in range(3):
        gath[0, i * 8 : i * 8 + 8] = mgot[pl.ds(i, 8, stride=8), :]
    spread = [
        copy(gath.at[0], gath.at[o], send_2.at[o], recv_2.at[o], {"lon": around[o - 1]})
        for o in range(1, 8)
    ]
    for hop in spread:
        hop.start()
    for halo in halos:
        halo.start()
    volume(stops[1], stops[2])

    @pl.when(early)
    def _():
        volume_product(dperm, trans, v_ref)

    def faces(g, t, remote):
        flux(g, t, remote, own, turn_ref, wf, terms)

    def from_below(t, m):
        return jnp.where(below_first, zero, pltpu.roll(own[5, t, m], 1, 1))

    def from_above(t, m):
        return jnp.where(above_last, zero, pltpu.roll(own[4, t, m], 127, 1))

    def radial(t, carry):
        faces(4, t, from_below)
        faces(5, t, from_above)
        return carry

    lax.fori_loop(0, 3, radial, 0)

    for hop in spread:
        hop.wait_recv()
    zout[...] = jnp.dot(
        chosen[...], gath[...].reshape(192, 128), precision=HIGH, preferred_element_type=F32
    )
    place = pl.ds(pl.multiple_of(z * 8, 8), 8)
    back = [
        copy(
            zout.at[o * 8 : o * 8 + 8], zrecv.at[place], send_3.at[o], recv_3.at[o],
            {"lon": along_z[o - 1]},
        )
        for o in range(1, 8)
    ]
    for hop in back:
        hop.start()
    zrecv[place, :] = zout[0:8, :]
    @pl.when(jnp.logical_not(early))
    def _():
        volume(stops[2], 8)
        volume_product(dperm, trans, v_ref)

    def inner_lon(index, carry):
        g = index // 2
        faces(g, index % 2 + 1 - g, lambda t, m: own[1 - g, t - 1 + 2 * g, m])
        return carry

    lax.fori_loop(0, 4, inner_lon, 0)
    halos[0].wait_recv()
    halos[1].wait_recv()

    def outer_lon(g, carry):
        faces(g, 2 * g, lambda t, m: rlon[g, m])
        return carry

    lax.fori_loop(0, 2, outer_lon, 0)

    @pl.when(has_south)
    def _():
        northward.wait_recv()

    @pl.when(has_north)
    def _():
        southward.wait_recv()

    def from_south(t, m):
        if m < 18:
            return pltpu.roll(jnp.where(upper, rs[t, m], own[3, t, m]), 64, 1)
        return jnp.where(upper, pltpu.roll(own[3, t, m], 64, 1), rs[t, m - 18])

    def from_north(t, m):
        if m < 18:
            return pltpu.roll(jnp.where(upper, own[2, t, m], rn[t, m]), 64, 1)
        return jnp.where(upper, rn[t, m - 18], pltpu.roll(own[2, t, m], 64, 1))

    def lats(t, carry):
        faces(2, t, from_south)
        faces(3, t, from_north)
        return carry

    lax.fori_loop(0, 3, lats, 0)
    for hop in back:
        hop.wait_recv()
    zon_ref[...] = zrecv[...]
    for sent in hops + halos + spread + back:
        sent.wait_send()

    @pl.when(has_north)
    def _():
        northward.wait_send()

    @pl.when(has_south)
    def _():
        southward.wait_send()


def exchange(*operands):
    vmem = pl.BlockSpec(memory_space=pltpu.VMEM)
    dma = pltpu.SemaphoreType.DMA
    return pl.pallas_call(
        kernel,
        out_shape=[
            jax.ShapeDtypeStruct((3, 6, 36, 8, 128), F32),
            jax.ShapeDtypeStruct((3, 1728, 128), F32),
            jax.ShapeDtypeStruct((64, 128), F32),
            jax.ShapeDtypeStruct((3, 12, 8, 128), F32),
        ],
        in_specs=[pl.BlockSpec(memory_space=pltpu.HBM)] * 2 + [vmem] * 6,
        out_specs=[vmem] * 4,
        scratch_shapes=[
            pltpu.VMEM((216, 3, 8, 128), BF16),
            pltpu.VMEM((216, 3, 8, 128), BF16),
            pltpu.VMEM((6, 3, 36, 16, 128), BF16),
            pltpu.VMEM((2, 36, 16, 128), BF16),
            pltpu.VMEM((3, 18, 16, 128), BF16),
            pltpu.VMEM((3, 18, 16, 128), BF16),
            pltpu.VMEM((3, 18, 16, 128), BF16),
            pltpu.VMEM((3, 18, 16, 128), BF16),
            pltpu.VMEM((3, 12, 16, 128), BF16),
            pltpu.VMEM((192, 512), F32),
            pltpu.VMEM((3, 32, 96), F32),
            pltpu.VMEM((216, 768), BF16),
            pltpu.VMEM((512, 768), BF16),
            pltpu.VMEM((512, 768), BF16),
            pltpu.VMEM((768, 3072), BF16),
            pltpu.VMEM((8, 384), F32),
            pltpu.VMEM((64, 192), F32),
            pltpu.VMEM((64, 128), F32),
            pltpu.VMEM((64, 128), F32),
            pltpu.VMEM((8, 24, 128), F32),
            pltpu.VMEM((64, 128), F32),
            pltpu.VMEM((64, 128), F32),
            dma((2,)), dma((4,)), dma((4,)), dma((8,)), dma((8,)), dma((8,)), dma((8,)), dma((8,)), dma((8,)),
        ],
        compiler_params=pltpu.CompilerParams(
            collective_id=0, has_side_effects=True, vmem_limit_bytes=VMEM_LIMIT
        ),
    )(*operands)


def finish_kernel(terms_in, v_ref, zon_ref, swaps, out_ref, terms):
    finish(swaps, terms_in, terms, zon_ref, v_ref, out_ref)


def finished(*operands):
    vmem = pl.BlockSpec(memory_space=pltpu.VMEM)
    return pl.pallas_call(
        finish_kernel,
        out_shape=jax.ShapeDtypeStruct((216, 3, 8, 128), BF16),
        in_specs=[vmem] * 4,
        out_specs=vmem,
        scratch_shapes=[pltpu.VMEM((3, 6, 36, 8, 128), F32)],
        compiler_params=pltpu.CompilerParams(vmem_limit_bytes=FINISH_LIMIT),
    )(*operands)


def body(state, adjoint, derivative, jac_tensor, jac_offset, zonal_kernel, face_numbers, orientation):
    s = jnp.transpose(state, (0, 2, 1, 3))
    a = jnp.transpose(adjoint, (0, 2, 1, 3))
    jac = jac_tensor.reshape(192, 8)
    off = jac_offset.reshape(24, 8)
    ring = zonal_kernel.reshape(1, 192)
    numbers = jnp.transpose(face_numbers, (0, 2, 1))
    turnings = jnp.transpose(orientation, (0, 2, 1))
    s, a, derivative, jac, off, ring, numbers, turnings = [
        pltpu.with_memory_space_constraint(x, pltpu.HBM)
        for x in (s, a, derivative, jac, off, ring, numbers, turnings)
    ]
    parts = exchange(s, a, derivative, jac, off, ring, numbers, turnings)
    out = finished(*parts)
    return jnp.transpose(out, (0, 2, 1, 3))


def solution(mesh):
    in_specs = (
        P(None, None, "lon", "lat"),
        P(None, None, "lon", "lat"),
        P(),
        P(),
        P(),
        P(),
        P("lon", "lat", None),
        P("lon", "lat", None),
    )
    out_specs = P(None, None, "lon", "lat")
    return jax.shard_map(body, mesh=mesh, in_specs=in_specs, out_specs=out_specs, check_vma=False)
```
